256 devices in a mesh: row: 16 (over y, z_hi, core), col: 16 (over x, z_lo).
Axes of the slice: x: 4, y: 4, z: 8 (z_hi: 2, z_lo: 4; z = z_hi * 4 + z_lo), core: 2. Of those that a mesh axis runs over, the one named last changes fastest.
Arguments:
- features: bfloat16 [32768, 1536], P(('row', 'col')), may hold values from -8 to 8
- targets: float32 [32768], P(('row', 'col')), may hold values from -6 to 6
- tile_pairs: int32 [16, 16, 32, 2], P('row', 'col'), may hold values from 0 to 15, as said below
- tile_count: int32 [16, 16], P('row', 'col'), may hold values from 1 to 32, as said below
Outputs:
- solution: float32 [32768], P(('row', 'col'))
- residual: float32 [32768], P(('row', 'col'))
The draws below stay inside these ranges and needn't reach their ends.
Inputs may be any that keep to these rules, and one draw needn't show every extreme that they name: `tile_pairs`: for each device the first tile_count slots name distinct local block pairs whose row block i is at most its column block j; over all devices each such pair is listed at most once; the first entry is below the number of devices along col, the second below the number along row; later slots hold any such numbers and are not used. `tile_count`: the device at row index 0 and the last col index always lists 32 tiles.
All inputs are finite; a program needn't handle non-finite values.
Results may differ from the reference program's by a relative error of at most 0.0003.
Values may be sent and summed in bfloat16 or wider, within the bound.
No kernel may reach another device: no remote copies, remote signals or barrier semaphores. Data moves between devices by JAX's collectives and lax.ppermute only.
A program may use at most 64 MiB of HBM per device.

```python
import jax
import jax.numpy as jnp
from jax import lax

D = 1536
BS = 128
ITERS = 2
SLOTS = 32
SAMPLES = 32768
N_ROW = 16
N_COL = 16


def pair_plan(key):
    total = N_ROW * N_COL
    count_key = jax.random.fold_in(key, 5)
    keys = jax.random.split(key, total)
    orders = jax.vmap(lambda subkey: jax.random.permutation(subkey, total))(keys)
    device = jnp.arange(total, dtype=jnp.int32)[:, None]
    device_row = device // N_COL
    device_col = device % N_COL
    flat = jnp.arange(total, dtype=jnp.int32)[None, :]
    local_row = flat // N_ROW
    local_col = flat % N_ROW
    first = device_row * N_COL + local_row
    second = local_col * N_COL + device_col
    usable = (first <= second).astype(jnp.int32)
    score = usable * total + orders.astype(jnp.int32)
    top_values, chosen = lax.top_k(score, SLOTS)
    pairs = jnp.stack([chosen // N_ROW, chosen % N_ROW], axis=-1).astype(jnp.int32)
    capacity = jnp.minimum(jnp.sum(usable, axis=-1), SLOTS).astype(jnp.int32)
    lower = (capacity + 1) // 2
    counts = jax.random.randint(count_key, (total,), lower, capacity + 1).astype(jnp.int32)
    full_device = N_COL - 1
    counts = jnp.where(jnp.arange(total, dtype=jnp.int32) == full_device, SLOTS, counts).astype(jnp.int32)
    return (pairs.reshape(N_ROW, N_COL, SLOTS, 2), counts.reshape(N_ROW, N_COL))


def draw_tile_pairs(key, part):
    return pair_plan(key)[0]


def draw_tile_count(key, part):
    return pair_plan(key)[1]


def draw_features(key, part):
    key = jax.random.fold_in(key, 11)
    centre_key, member_key, noise_key = jax.random.split(key, 3)
    centre_count = 32
    member = jax.random.randint(member_key, (SAMPLES,), 0, centre_count)
    centres = jax.random.normal(centre_key, (centre_count, D), jnp.float32)
    noise = 0.63 * jax.random.normal(noise_key, (SAMPLES, D), jnp.float32)
    values = centres[member] + noise
    return jnp.clip(values, -8.0, 8.0).astype(jnp.bfloat16)


def block_levels(own_key, dims, cuts, least, high):
    def one(axis_at, shards_of):
        draws = jax.random.uniform(jax.random.fold_in(jax.random.fold_in(own_key, 6), axis_at), (shards_of,), jnp.float32, least / len(cuts), high / len(cuts))
        return jnp.repeat(jnp.exp(draws), dims[axis_at] // shards_of).reshape((-1,) + (1,) * (len(dims) - axis_at - 1))

    gain = one(*cuts[0])
    for cut in cuts[1:]:
        gain = gain * one(*cut)
    return gain


def normal_values(stream_key, extent, deviation, limit, pieces=(), kind=jnp.bfloat16):
    entries = deviation * jax.random.normal(stream_key, extent, jnp.float32)
    if pieces:
        entries = entries * block_levels(stream_key, extent, pieces, -0.22, 0.18)
    return jnp.clip(entries, -limit, limit).astype(kind)


def setup_inputs(seed: int = 0) -> dict:
    key_of = jax.random.split(jax.random.key(seed), 5)
    features = draw_features(jax.random.fold_in(key_of[4], 71), 0)
    targets = normal_values(key_of[1], (SAMPLES,), 1.0, 6.0, ((0, 256),), jnp.float32)
    tile_pairs = draw_tile_pairs(jax.random.fold_in(key_of[4], 71), 0)
    tile_count = draw_tile_count(jax.random.fold_in(key_of[4], 71), 0)
    return {"features": features, "targets": targets, "tile_pairs": tile_pairs, "tile_count": tile_count}


RIDGE = 1.0
GROUP = 4


def reference(features, targets, tile_pairs, tile_count):
    blocks = features.reshape(N_ROW * N_COL, BS, D).astype(jnp.float32)
    norms = jnp.sum(blocks * blocks, axis=2)
    device_row = jnp.arange(N_ROW, dtype=jnp.int32)[:, None, None]
    device_col = jnp.arange(N_COL, dtype=jnp.int32)[None, :, None]
    first = (device_row * N_COL + tile_pairs[..., 0]).astype(jnp.int32)
    second = (tile_pairs[..., 1] * N_COL + device_col).astype(jnp.int32)
    slot_index = jnp.arange(SLOTS, dtype=jnp.int32)[None, None, :]
    live = (slot_index < tile_count[:, :, None]).astype(jnp.float32)
    other = live * (first != second).astype(jnp.float32)
    first_groups = first.reshape(-1, GROUP)
    second_groups = second.reshape(-1, GROUP)
    live_groups = live.reshape(-1, GROUP)
    other_groups = other.reshape(-1, GROUP)

    def sweep(vector):
        vector_blocks = vector.reshape(-1, BS)

        def advance(carry, group):
            result, degree = carry
            take_row, take_col, live_now, other_now = group
            left = blocks[take_row]
            right = blocks[take_col]
            inner = jnp.einsum('gid,gjd->gij', left, right, precision=lax.Precision.HIGHEST)
            distance = norms[take_row][:, :, None] + norms[take_col][:, None, :] - 2.0 * inner
            kernel = jnp.exp(-jnp.maximum(distance, 0.0) / D)
            row_term = jnp.einsum('gij,gj->gi', kernel, vector_blocks[take_col], precision=lax.Precision.HIGHEST) * live_now[:, None]
            col_term = jnp.einsum('gij,gi->gj', kernel, vector_blocks[take_row], precision=lax.Precision.HIGHEST) * other_now[:, None]
            result = result.at[take_row].add(row_term).at[take_col].add(col_term)
            degree = degree.at[take_row].add(jnp.sum(kernel, axis=2) * live_now[:, None])
            degree = degree.at[take_col].add(jnp.sum(kernel, axis=1) * other_now[:, None])
            return (result, degree), None

        zeros = jnp.zeros((N_ROW * N_COL, BS), jnp.float32)
        outcome = lax.scan(advance, (zeros, zeros), (first_groups, second_groups, live_groups, other_groups))
        result, degree = outcome[0]
        return result.reshape(-1), degree.reshape(-1)

    solution = jnp.zeros_like(targets)
    residual = targets
    direction = targets
    norm_now = jnp.sum(residual * residual)
    degree = jnp.zeros_like(targets)
    for counter in range(ITERS):
        product, degree_now = sweep(direction)
        if counter == 0:
            degree = degree_now
        image = RIDGE * direction + (degree * direction + product) / BS
        alpha = norm_now / jnp.sum(direction * image)
        solution = solution + alpha * direction
        residual = residual - alpha * image
        norm_next = jnp.sum(residual * residual)
        direction = residual + (norm_next / norm_now) * direction
        norm_now = norm_next
    return solution, residual
```

```python
import jax
import jax.numpy as jnp
from jax import lax
from jax.experimental import pallas as pl
from jax.experimental.pallas import tpu as pltpu
from jax.sharding import PartitionSpec as P

RIDGE = 1.0
GROUP = 4
AXES = ("row", "col")
LANES = 128
VMEM_BYTES = 40 * 1024 * 1024


def spread_columns(values, out_ref):
    turned = jnp.transpose(values)
    for k in range(values.shape[0]):
        out_ref[k] = jnp.broadcast_to(turned[:, k : k + 1], (LANES, LANES))


def write_slots(row_acc, col_acc, row_index, col_index, n_row, n_col, out_ref):
    out_ref[...] = jnp.zeros_like(out_ref)
    lane = lax.broadcasted_iota(jnp.int32, (LANES, LANES), 1)
    packed = jnp.zeros((LANES, LANES), jnp.float32)
    for a in range(n_col):
        column = jnp.sum(row_acc[a], axis=1, keepdims=True)
        packed = packed + jnp.where(lane == a, column, 0.0)
    first = pl.multiple_of(row_index * n_col, n_col)
    out_ref[pl.ds(first, n_col), :] = jnp.transpose(packed)[0:n_col, :]
    for b in range(n_row):
        at = pl.ds(b * n_col + col_index, 1)
        out_ref[at, :] = out_ref[at, :] + jnp.sum(col_acc[b], axis=0, keepdims=True)


def add_tile(kernel, slot, vec_ref, spread_ref, row_acc, col_acc, where, pairs, listed, n_col):
    row_index, col_index = where
    a = pairs[slot, 0]
    b = pairs[slot, 1]
    j = b * n_col + col_index
    live = jnp.where(slot < listed, 1.0, 0.0)
    other = jnp.where(row_index * n_col + a == j, 0.0, live)
    both = kernel * (spread_ref[a] + vec_ref[pl.ds(j, 1), :])
    row_acc[a] = row_acc[a] + both * live
    col_acc[b] = col_acc[b] + jnp.sum(both.reshape(16, 8, LANES), axis=0) * other


def first_sweep_kernel(
    place, pairs, count, rows_ref, cols_ref, known_ref, kernel_ref, out_ref,
    vec, norms, spread_v, spread_n, row_acc, col_acc,
):
    n_col = rows_ref.shape[0]
    n_row = cols_ref.shape[0]
    width = rows_ref.shape[2]
    row_index = place[0]
    col_index = place[1]
    listed = count[0]
    first = pl.multiple_of(row_index * n_col, n_col)
    vec[...] = known_ref[:, 0:LANES]
    norms[...] = known_ref[:, LANES : 2 * LANES]
    spread_columns(vec[pl.ds(first, n_col), :], spread_v)
    spread_columns(norms[pl.ds(first, n_col), :], spread_n)
    row_acc[...] = jnp.zeros_like(row_acc)
    col_acc[...] = jnp.zeros_like(col_acc)

    def step(turn, carry):
        for g in range(GROUP):
            slot = turn * GROUP + g
            a = pairs[slot, 0]
            b = pairs[slot, 1]
            inner = lax.dot_general(
                rows_ref[a], cols_ref[b], (((1,), (1,)), ((), ())),
                preferred_element_type=jnp.float32,
            )
            norm_j = norms[pl.ds(b * n_col + col_index, 1), :]
            distance = spread_n[a] + norm_j - 2.0 * inner
            kernel = jnp.exp(jnp.maximum(distance, 0.0) * (-1.0 / width))
            kernel_ref[slot] = kernel
            add_tile(
                kernel, slot, vec, spread_v, row_acc, col_acc,
                (row_index, col_index), pairs, listed, n_col,
            )
        return carry

    lax.fori_loop(0, pairs.shape[0] // GROUP, step, 0)
    write_slots(row_acc, col_acc, row_index, col_index, n_row, n_col, out_ref)


def second_sweep_kernel(
    place, pairs, count, kernel_ref, start_ref, image_ref, out_ref, own_ref,
    next_dir, sums, spread_v, row_acc, col_acc, *, n_row, n_col,
):
    row_index = place[0]
    col_index = place[1]
    listed = count[0]
    start = start_ref[...]
    image = image_ref[...]
    norm_0 = jnp.sum(start * start)
    alpha = norm_0 / jnp.sum(start * image)
    residual = start - alpha * image
    norm_1 = jnp.sum(residual * residual)
    direction = residual + (norm_1 / norm_0) * start
    next_dir[...] = direction
    first = pl.multiple_of(row_index * n_col, n_col)
    spread_columns(next_dir[pl.ds(first, n_col), :], spread_v)
    row_acc[...] = jnp.zeros_like(row_acc)
    col_acc[...] = jnp.zeros_like(col_acc)

    def step(turn, carry):
        for g in range(GROUP):
            slot = turn * GROUP + g
            add_tile(
                kernel_ref[slot], slot, next_dir, spread_v, row_acc, col_acc,
                (row_index, col_index), pairs, listed, n_col,
            )
        return carry

    lax.fori_loop(0, pairs.shape[0] // GROUP, step, 0)
    write_slots(row_acc, col_acc, row_index, col_index, n_row, n_col, sums)
    partial = jnp.sum(sums[...] * next_dir[...])
    out_ref[:, 0:LANES] = sums[...]
    out_ref[:, LANES : 2 * LANES] = jnp.full((n_row * n_col, LANES), partial, jnp.float32)
    mine = pl.ds(row_index * n_col + col_index, 1)
    own_start = start_ref[mine, :]
    own_dir = next_dir[mine, :]
    own_ref[0:1, :] = alpha * own_start
    own_ref[1:2, :] = own_start - alpha * image_ref[mine, :]
    own_ref[2:3, :] = own_dir
    own_ref[3:4, :] = jnp.full((1, LANES), norm_1, jnp.float32)
    own_ref[4:5, :] = jnp.full((1, LANES), jnp.sum(direction * direction), jnp.float32)
    own_ref[5:8, :] = jnp.zeros((3, LANES), jnp.float32)


def image_kernel(place, partial_ref, own_ref, out_ref, *, block):
    total = jnp.sum(partial_ref[...], axis=0, keepdims=True)
    image = RIDGE * own_ref[...] + total * (1.0 / block)
    out_ref[...] = jnp.broadcast_to(image, out_ref.shape)


def finish_kernel(partial_ref, own_ref, solution_ref, residual_ref, *, block):
    total = jnp.sum(partial_ref[...], axis=0, keepdims=True)
    direction = own_ref[2:3, :]
    image = RIDGE * direction + total[:, 0:LANES] * (1.0 / block)
    against = RIDGE * own_ref[4:5, :] + total[:, LANES : 2 * LANES] * (1.0 / block)
    alpha = own_ref[3:4, :] / against
    solution_ref[...] = own_ref[0:1, :] + alpha * direction
    residual_ref[...] = own_ref[1:2, :] - alpha * image


def swap(slots):
    return lax.all_to_all(slots, AXES, 0, 0, tiled=True)


VM = pl.BlockSpec(memory_space=pltpu.VMEM)
SM = pl.BlockSpec(memory_space=pltpu.SMEM)


def body(features, targets, tile_pairs, tile_count):
    n_row = lax.axis_size("row")
    n_col = lax.axis_size("col")
    total = n_row * n_col
    place = jnp.stack([lax.axis_index("row"), lax.axis_index("col")]).astype(jnp.int32)
    pairs = tile_pairs[0, 0]
    count = tile_count[0]
    slots = pairs.shape[0]
    block, width = features.shape
    params = pltpu.CompilerParams(vmem_limit_bytes=VMEM_BYTES)
    f32 = jnp.float32

    wide = features.astype(f32)
    norms = jnp.sum(wide * wide, axis=1)
    mine = jnp.concatenate([targets, norms])[None, :]
    known = swap(jnp.broadcast_to(mine, (total, 2 * block)))

    rows = lax.all_gather(features, "col", axis=0).reshape(n_col, block, width)
    cols = lax.all_gather(features, "row", axis=0).reshape(n_row, block, width)

    accumulators = [
        pltpu.VMEM((n_col, block, block), f32),
        pltpu.VMEM((n_row, 8, block), f32),
    ]
    kernel, partial = pl.pallas_call(
        first_sweep_kernel,
        out_shape=(
            jax.ShapeDtypeStruct((slots, block, block), f32),
            jax.ShapeDtypeStruct((total, block), f32),
        ),
        in_specs=[SM, SM, SM, VM, VM, VM],
        out_specs=(VM, VM),
        scratch_shapes=[pltpu.VMEM((total, block), f32)] * 2
        + [pltpu.VMEM((n_col, block, block), f32)] * 2 + accumulators,
        compiler_params=params,
    )(place, pairs, count, rows, cols, known)

    image = pl.pallas_call(
        lambda *refs: image_kernel(None, *refs, block=block),
        out_shape=jax.ShapeDtypeStruct((total, block), f32),
        in_specs=[VM, VM],
        out_specs=VM,
        compiler_params=params,
    )(swap(partial), targets[None, :])
    images = swap(image)

    partial_2, own = pl.pallas_call(
        lambda *refs: second_sweep_kernel(*refs, n_row=n_row, n_col=n_col),
        out_shape=(
            jax.ShapeDtypeStruct((total, 2 * block), f32),
            jax.ShapeDtypeStruct((8, block), f32),
        ),
        in_specs=[SM, SM, SM, VM, VM, VM],
        out_specs=(VM, VM),
        scratch_shapes=[
            pltpu.VMEM((total, block), f32),
            pltpu.VMEM((total, block), f32),
            pltpu.VMEM((n_col, block, block), f32),
        ] + accumulators,
        compiler_params=params,
    )(place, pairs, count, kernel, known[:, 0:block], images)

    result, residual = pl.pallas_call(
        lambda *refs: finish_kernel(*refs, block=block),
        out_shape=(jax.ShapeDtypeStruct((1, block), f32),) * 2,
        in_specs=[VM, VM],
        out_specs=(VM, VM),
        compiler_params=params,
    )(swap(partial_2), own)
    return (result[0], residual[0])


def solution(mesh):
    return jax.shard_map(
        body,
        mesh=mesh,
        in_specs=(
            P(("row", "col"), None),
            P(("row", "col")),
            P("row", "col", None, None),
            P("row", "col"),
        ),
        out_specs=(P(("row", "col")), P(("row", "col"))),
        check_vma=False,
    )
```

```python
import jax
import jax.numpy as jnp
import numpy as np
from jax import lax
from jax.experimental import pallas as pl
from jax.experimental.pallas import tpu as pltpu
from jax.sharding import PartitionSpec as P

RIDGE = 1.0
GROUP = 4
AXES = ("row", "col")
LANES = 128
VMEM_BYTES = 40 * 1024 * 1024


def spread_columns(values, out_ref):
    turned = jnp.transpose(values)
    for k in range(values.shape[0]):
        out_ref[k] = jnp.broadcast_to(turned[:, k : k + 1], (LANES, LANES))


def write_slots(row_acc, col_acc, row_index, col_index, n_row, n_col, out_ref):
    out_ref[...] = jnp.zeros_like(out_ref)
    lane = lax.broadcasted_iota(jnp.int32, (LANES, LANES), 1)
    packed = jnp.zeros((LANES, LANES), jnp.float32)
    for a in range(n_col):
        column = jnp.sum(row_acc[a], axis=1, keepdims=True)
        packed = packed + jnp.where(lane == a, column, 0.0)
    first = pl.multiple_of(row_index * n_col, n_col)
    out_ref[pl.ds(first, n_col), :] = jnp.transpose(packed)[0:n_col, :]
    for b in range(n_row):
        at = pl.ds(b * n_col + col_index, 1)
        out_ref[at, :] = out_ref[at, :] + jnp.sum(col_acc[b], axis=0, keepdims=True)


def add_tile(kernel, slot, vec_ref, spread_ref, row_acc, col_acc, where, pairs, listed, n_col):
    row_index, col_index = where
    a = pairs[slot, 0]
    b = pairs[slot, 1]
    j = b * n_col + col_index
    live = jnp.where(slot < listed, 1.0, 0.0)
    other = jnp.where(row_index * n_col + a == j, 0.0, live)
    both = kernel * (spread_ref[a] + vec_ref[pl.ds(j, 1), :])
    row_acc[a] = row_acc[a] + both * live
    col_acc[b] = col_acc[b] + jnp.sum(both.reshape(16, 8, LANES), axis=0) * other


def first_sweep_kernel(
    row_plan, col_plan, place, pairs, count, row_spot, col_spot, known_ref, *rest
):
    n_pieces = len(row_plan) + len(col_plan)
    pieces = rest[:n_pieces]
    (kernel_ref, out_ref, rows_ref, cols_ref, sems, vec, norms, spread_v, spread_n,
     row_acc, col_acc) = rest[n_pieces:]
    n_col = rows_ref.shape[0]
    n_row = cols_ref.shape[0]
    width = rows_ref.shape[2]
    copies = []
    for k, (index, low, high) in enumerate(row_plan + col_plan):
        target = rows_ref if k < len(row_plan) else cols_ref
        copy = pltpu.make_async_copy(pieces[k], target.at[index, low:high], sems.at[k])
        copy.start()
        copies.append(copy)
    row_index = place[0]
    col_index = place[1]
    listed = count[0]
    first = pl.multiple_of(row_index * n_col, n_col)
    vec[...] = known_ref[:, 0:LANES]
    norms[...] = known_ref[:, LANES : 2 * LANES]
    spread_columns(vec[pl.ds(first, n_col), :], spread_v)
    spread_columns(norms[pl.ds(first, n_col), :], spread_n)
    row_acc[...] = jnp.zeros_like(row_acc)
    col_acc[...] = jnp.zeros_like(col_acc)

    for copy in copies:
        copy.wait()

    def step(turn, carry):
        for g in range(GROUP):
            slot = turn * GROUP + g
            a = pairs[slot, 0]
            b = pairs[slot, 1]
            inner = lax.dot_general(
                rows_ref[row_spot[col_index, a]], cols_ref[col_spot[row_index, b]], (((1,), (1,)), ((), ())),
                preferred_element_type=jnp.float32,
            )
            norm_j = norms[pl.ds(b * n_col + col_index, 1), :]
            distance = spread_n[a] + norm_j - 2.0 * inner
            kernel = jnp.exp(jnp.maximum(distance, 0.0) * (-1.0 / width))
            kernel_ref[slot] = kernel
            add_tile(
                kernel, slot, vec, spread_v, row_acc, col_acc,
                (row_index, col_index), pairs, listed, n_col,
            )
        return carry

    lax.fori_loop(0, pairs.shape[0] // GROUP, step, 0)
    write_slots(row_acc, col_acc, row_index, col_index, n_row, n_col, out_ref)


def second_sweep_kernel(
    place, pairs, count, kernel_ref, start_ref, image_ref, out_ref, own_ref,
    next_dir, sums, spread_v, row_acc, col_acc, *, n_row, n_col,
):
    row_index = place[0]
    col_index = place[1]
    listed = count[0]
    start = start_ref[...]
    image = image_ref[...]
    norm_0 = jnp.sum(start * start)
    alpha = norm_0 / jnp.sum(start * image)
    residual = start - alpha * image
    norm_1 = jnp.sum(residual * residual)
    direction = residual + (norm_1 / norm_0) * start
    next_dir[...] = direction
    first = pl.multiple_of(row_index * n_col, n_col)
    spread_columns(next_dir[pl.ds(first, n_col), :], spread_v)
    row_acc[...] = jnp.zeros_like(row_acc)
    col_acc[...] = jnp.zeros_like(col_acc)

    def step(turn, carry):
        for g in range(GROUP):
            slot = turn * GROUP + g
            add_tile(
                kernel_ref[slot], slot, next_dir, spread_v, row_acc, col_acc,
                (row_index, col_index), pairs, listed, n_col,
            )
        return carry

    lax.fori_loop(0, pairs.shape[0] // GROUP, step, 0)
    write_slots(row_acc, col_acc, row_index, col_index, n_row, n_col, sums)
    partial = jnp.sum(sums[...] * next_dir[...])
    out_ref[:, 0:LANES] = sums[...]
    out_ref[:, LANES : 2 * LANES] = jnp.full((n_row * n_col, LANES), partial, jnp.float32)
    mine = pl.ds(row_index * n_col + col_index, 1)
    own_start = start_ref[mine, :]
    own_dir = next_dir[mine, :]
    own_ref[0:1, :] = alpha * own_start
    own_ref[1:2, :] = own_start - alpha * image_ref[mine, :]
    own_ref[2:3, :] = own_dir
    own_ref[3:4, :] = jnp.full((1, LANES), norm_1, jnp.float32)
    own_ref[4:5, :] = jnp.full((1, LANES), jnp.sum(direction * direction), jnp.float32)
    own_ref[5:8, :] = jnp.zeros((3, LANES), jnp.float32)


def image_kernel(place, partial_ref, own_ref, out_ref, *, block):
    total = jnp.sum(partial_ref[...], axis=0, keepdims=True)
    image = RIDGE * own_ref[...] + total * (1.0 / block)
    out_ref[...] = jnp.broadcast_to(image, out_ref.shape)


def finish_kernel(partial_ref, own_ref, solution_ref, residual_ref, *, block):
    total = jnp.sum(partial_ref[...], axis=0, keepdims=True)
    direction = own_ref[2:3, :]
    image = RIDGE * direction + total[:, 0:LANES] * (1.0 / block)
    against = RIDGE * own_ref[4:5, :] + total[:, LANES : 2 * LANES] * (1.0 / block)
    alpha = own_ref[3:4, :] / against
    solution_ref[...] = own_ref[0:1, :] + alpha * direction
    residual_ref[...] = own_ref[1:2, :] - alpha * image


def swap(slots):
    return lax.all_to_all(slots, AXES, 0, 0, tiled=True)


VM = pl.BlockSpec(memory_space=pltpu.VMEM)
SM = pl.BlockSpec(memory_space=pltpu.SMEM)
ANY = pl.BlockSpec(memory_space=pl.ANY)
NX, NZ = 4, 4
NY, NH, NK = 4, 2, 2
Z_ORDER = ((0, 1, 2, 3), (1, 0, 2, 3), (2, 1, 3, 0), (3, 2, 1, 0))


def along_x(array, step):
    pairs = [(x * NZ + z, (x + step) % NX * NZ + z) for x in range(NX) for z in range(NZ)]
    return lax.ppermute(array, "col", pairs)


def along_z(array, step):
    pairs = [
        (x * NZ + z, x * NZ + z + step) for x in range(NX) for z in range(NZ) if 0 <= z + step < NZ
    ]
    return lax.ppermute(array, "col", pairs)


def along_row(array, step, half, core):
    pairs = []
    for y in range(NY):
        for h in range(NH):
            for k in range(NK):
                to = ((y + step) % NY * NH + (h + half) % NH) * NK + (k + core) % NK
                pairs.append(((y * NH + h) * NK + k, to))
    return lax.ppermute(array, "row", pairs)


def ring(array, send):
    middle = array.shape[-2] // 2
    before = send(array, 1)
    after = send(array, -1)
    far_low = send(before[..., :middle, :], 1)
    far_high = send(after[..., middle:, :], -1)
    return before, after, far_low, far_high


def gather_rows(features):
    block = features.shape[0]
    z = lax.axis_index("col") % NZ
    up1 = along_z(features, 1)
    down1 = along_z(features, -1)
    up2 = along_z(up1, 1)
    down2 = along_z(down1, -1)
    up3 = along_z(up2, 1)
    down3 = along_z(down2, -1)
    kept = [
        features,
        jnp.where(z == 0, down1, up1),
        jnp.where(z == 0, down2, jnp.where(z == 3, up2, down1)),
        jnp.where(z == 0, down3, jnp.where(z == 1, down2, jnp.where(z == 2, up2, up3))),
    ]
    pieces, plan = [], []
    for m, array in enumerate(kept):
        before, after, far_low, far_high = ring(array, along_x)
        pieces += [array, before, after, far_low, far_high]
        plan += [
            (m, 0, block), (3 * NZ + m, 0, block), (NZ + m, 0, block),
            (2 * NZ + m, 0, block // 2), (2 * NZ + m, block // 2, block),
        ]
    return pieces, plan


def gather_cols(features):
    block = features.shape[0]
    across = along_row(features, 0, 1, 0)
    both = jnp.stack([features, across])
    before, after, far_low, far_high = ring(both, lambda array, step: along_row(array, step, 0, 0))
    pieces = [both, before, after, far_low, far_high]
    plan = [
        (slice(0, 2), 0, block), (slice(6, 8), 0, block), (slice(2, 4), 0, block),
        (slice(4, 6), 0, block // 2), (slice(4, 6), block // 2, block),
    ]
    pieces += [along_row(piece, 0, 0, 1) for piece in pieces]
    plan += [(slice(at.start + 8, at.stop + 8), low, high) for at, low, high in plan]
    return pieces, plan


def spots():
    row_spot = np.zeros((NX * NZ, NX * NZ), np.int32)
    for x in range(NX):
        for z in range(NZ):
            for ax in range(NX):
                for az in range(NZ):
                    row_spot[x * NZ + z, ax * NZ + az] = (ax - x) % NX * NZ + Z_ORDER[z].index(az)
    col_spot = np.zeros((NY * NH * NK,) * 2, np.int32)
    for here in range(NY * NH * NK):
        for there in range(NY * NH * NK):
            dy = (there // 4 - here // 4) % NY
            dh = (there // 2 - here // 2) % 2
            dk = (there - here) % 2
            col_spot[here, there] = dk * 8 + dy * 2 + dh
    return jnp.asarray(row_spot), jnp.asarray(col_spot)


def body(features, targets, tile_pairs, tile_count):
    n_row = lax.axis_size("row")
    n_col = lax.axis_size("col")
    total = n_row * n_col
    place = jnp.stack([lax.axis_index("row"), lax.axis_index("col")]).astype(jnp.int32)
    pairs = tile_pairs[0, 0]
    count = tile_count[0]
    slots = pairs.shape[0]
    block, width = features.shape
    params = pltpu.CompilerParams(vmem_limit_bytes=VMEM_BYTES)
    f32 = jnp.float32

    wide = features.astype(f32)
    norms = jnp.sum(wide * wide, axis=1)
    mine = jnp.concatenate([targets, norms])[None, :]
    known = swap(jnp.broadcast_to(mine, (total, 2 * block)))

    row_pieces, row_plan = gather_rows(features)
    col_pieces, col_plan = gather_cols(features)
    row_spot, col_spot = spots()

    accumulators = [
        pltpu.VMEM((n_col, block, block), f32),
        pltpu.VMEM((n_row, 8, block), f32),
    ]
    kernel, partial = pl.pallas_call(
        lambda *refs: first_sweep_kernel(row_plan, col_plan, *refs),
        out_shape=(
            jax.ShapeDtypeStruct((slots, block, block), f32),
            jax.ShapeDtypeStruct((total, block), f32),
        ),
        in_specs=[SM, SM, SM, SM, SM, VM] + [ANY] * (len(row_plan) + len(col_plan)),
        out_specs=(VM, VM),
        scratch_shapes=[
            pltpu.VMEM((n_col, block, width), jnp.bfloat16),
            pltpu.VMEM((n_row, block, width), jnp.bfloat16),
            pltpu.SemaphoreType.DMA((len(row_plan) + len(col_plan),)),
        ]
        + [pltpu.VMEM((total, block), f32)] * 2
        + [pltpu.VMEM((n_col, block, block), f32)] * 2 + accumulators,
        compiler_params=params,
    )(place, pairs, count, row_spot, col_spot, known, *row_pieces, *col_pieces)

    image = pl.pallas_call(
        lambda *refs: image_kernel(None, *refs, block=block),
        out_shape=jax.ShapeDtypeStruct((total, block), f32),
        in_specs=[VM, VM],
        out_specs=VM,
        compiler_params=params,
    )(swap(partial), targets[None, :])
    images = swap(image)

    partial_2, own = pl.pallas_call(
        lambda *refs: second_sweep_kernel(*refs, n_row=n_row, n_col=n_col),
        out_shape=(
            jax.ShapeDtypeStruct((total, 2 * block), f32),
            jax.ShapeDtypeStruct((8, block), f32),
        ),
        in_specs=[SM, SM, SM, VM, VM, VM],
        out_specs=(VM, VM),
        scratch_shapes=[
            pltpu.VMEM((total, block), f32),
            pltpu.VMEM((total, block), f32),
            pltpu.VMEM((n_col, block, block), f32),
        ] + accumulators,
        compiler_params=params,
    )(place, pairs, count, kernel, known[:, 0:block], images)

    result, residual = pl.pallas_call(
        lambda *refs: finish_kernel(*refs, block=block),
        out_shape=(jax.ShapeDtypeStruct((1, block), f32),) * 2,
        in_specs=[VM, VM],
        out_specs=(VM, VM),
        compiler_params=params,
    )(swap(partial_2), own)
    return (result[0], residual[0])


def solution(mesh):
    return jax.shard_map(
        body,
        mesh=mesh,
        in_specs=(
            P(("row", "col"), None),
            P(("row", "col")),
            P("row", "col", None, None),
            P("row", "col"),
        ),
        out_specs=(P(("row", "col")), P(("row", "col"))),
        check_vma=False,
    )
```

```python
import jax
import jax.numpy as jnp
import numpy as np
from jax import lax
from jax.experimental import pallas as pl
from jax.experimental.pallas import tpu as pltpu
from jax.sharding import PartitionSpec as P

RIDGE = 1.0
GROUP = 4
AXES = ("row", "col")
LANES = 128
LARGE = 58 * 1024 * 1024
SMALL = 8 * 1024 * 1024


def spread_columns(values, out_ref):
    turned = jnp.transpose(values)
    for k in range(values.shape[0]):
        out_ref[k] = jnp.broadcast_to(turned[:, k : k + 1], (LANES, LANES))


def write_slots(row_acc, col_acc, row_index, col_index, n_row, n_col, out_ref):
    out_ref[...] = jnp.zeros_like(out_ref)
    lane = lax.broadcasted_iota(jnp.int32, (LANES, LANES), 1)
    packed = jnp.zeros((LANES, LANES), jnp.float32)
    for a in range(n_col):
        column = jnp.sum(row_acc[a], axis=1, keepdims=True)
        packed = packed + jnp.where(lane == a, column, 0.0)
    first = pl.multiple_of(row_index * n_col, n_col)
    out_ref[pl.ds(first, n_col), :] = jnp.transpose(packed)[0:n_col, :]
    for b in range(n_row):
        at = pl.ds(b * n_col + col_index, 1)
        out_ref[at, :] = out_ref[at, :] + jnp.sum(col_acc[b], axis=0, keepdims=True)


def split3(value):
    high = value.astype(jnp.bfloat16)
    rest = value - high.astype(jnp.float32)
    middle = rest.astype(jnp.bfloat16)
    return high, middle, (rest - middle.astype(jnp.float32)).astype(jnp.bfloat16)


def pack_kernel(features_ref, targets_ref, out_ref):
    width = features_ref.shape[1]
    wide = features_ref[...].astype(jnp.float32)
    norm = jnp.broadcast_to(jnp.sum(wide * wide, axis=1, keepdims=True), (LANES, LANES))
    target = jnp.transpose(jnp.broadcast_to(targets_ref[...], (LANES, LANES)))
    lane = lax.broadcasted_iota(jnp.int32, (LANES, LANES), 1)
    extra = jnp.zeros((LANES, LANES), jnp.float32)
    for k, part in enumerate(split3(target) + split3(norm)):
        extra = jnp.where(lane == k, part.astype(jnp.float32), extra)
    out_ref[:, 0:width] = features_ref[...]
    out_ref[:, width : width + LANES] = extra.astype(jnp.bfloat16)


def add_tile(kernel, slot, spread, across, row_acc, col_acc, where, pairs, listed, n_col):
    row_index, col_index = where
    a = pairs[slot, 0]
    b = pairs[slot, 1]
    live = jnp.where(slot < listed, 1.0, 0.0)
    other = jnp.where(row_index * n_col + a == b * n_col + col_index, 0.0, live)
    both = kernel * (spread + across)
    row_acc[a] = row_acc[a] + both * live
    col_acc[b] = col_acc[b] + jnp.sum(both.reshape(16, 8, LANES), axis=0) * other


def first_sweep_kernel(
    row_plan, col_plan, width, place, pairs, count, row_spot, col_spot, *rest
):
    n_pieces = len(row_plan) + len(col_plan)
    pieces = rest[:n_pieces]
    (kernel_ref, out_ref, held, held_sems, rows_ref, cols_ref, sems, vec, norms,
     spread_v, spread_n, row_acc, col_acc) = rest[n_pieces:]
    n_col = rows_ref.shape[0]
    n_row = cols_ref.shape[0]
    copies = []
    for k, taken in enumerate(row_plan + col_plan):
        target = rows_ref if k < len(row_plan) else cols_ref
        for index, part in taken:
            source = pieces[k] if part is None else pieces[k].at[part]
            copy = pltpu.make_async_copy(source, target.at[index], sems.at[len(copies)])
            copy.start()
            copies.append(copy)
    row_index = place[0]
    col_index = place[1]
    listed = count[0]
    row_acc[...] = jnp.zeros_like(row_acc)
    col_acc[...] = jnp.zeros_like(col_acc)
    for copy in copies:
        copy.wait()
    for k in range(n_col):
        extra = rows_ref[k, :, width : width + LANES].astype(jnp.float32)
        value = extra[:, 0:1] + (extra[:, 1:2] + extra[:, 2:3])
        spread_v[k] = jnp.broadcast_to(value, (LANES, LANES))
        value = extra[:, 3:4] + (extra[:, 4:5] + extra[:, 5:6])
        spread_n[k] = jnp.broadcast_to(value, (LANES, LANES))
    for k in range(n_row):
        extra = jnp.transpose(cols_ref[k, :, width : width + LANES].astype(jnp.float32))
        vec[k : k + 1, :] = extra[0:1, :] + (extra[1:2, :] + extra[2:3, :])
        norms[k : k + 1, :] = extra[3:4, :] + (extra[4:5, :] + extra[5:6, :])

    def step(turn, carry):
        for g in range(GROUP):
            slot = turn * GROUP + g
            a = row_spot[pairs[slot, 0]]
            b = col_spot[pairs[slot, 1]]
            inner = lax.dot_general(
                rows_ref[a, :, 0:width], cols_ref[b, :, 0:width], (((1,), (1,)), ((), ())),
                preferred_element_type=jnp.float32,
            )
            distance = spread_n[a] + norms[pl.ds(b, 1), :] - 2.0 * inner
            kernel = jnp.exp(jnp.maximum(distance, 0.0) * (-1.0 / width))
            held[slot] = kernel
            add_tile(
                kernel, slot, spread_v[a], vec[pl.ds(b, 1), :], row_acc, col_acc,
                (row_index, col_index), pairs, listed, n_col,
            )
        return carry

    lax.fori_loop(0, pairs.shape[0] // GROUP, step, 0)
    save = pltpu.make_async_copy(held, kernel_ref, held_sems.at[0])
    save.start()
    write_slots(row_acc, col_acc, row_index, col_index, n_row, n_col, out_ref)
    save.wait()


def second_sweep_kernel(
    place, pairs, count, kernel_ref, known_ref, out_ref, own_ref,
    held, held_sems, start_ref, image_ref, next_dir, sums, spread_v, row_acc, col_acc,
    *, n_row, n_col,
):
    fetch = pltpu.make_async_copy(kernel_ref, held, held_sems.at[0])
    fetch.start()
    row_index = place[0]
    col_index = place[1]
    listed = count[0]
    image = known_ref[:, 0:LANES]
    start = known_ref[:, LANES : 2 * LANES]
    image_ref[...] = image
    start_ref[...] = start
    norm_0 = jnp.sum(start * start)
    alpha = norm_0 / jnp.sum(start * image)
    residual = start - alpha * image
    norm_1 = jnp.sum(residual * residual)
    direction = residual + (norm_1 / norm_0) * start
    next_dir[...] = direction
    first = pl.multiple_of(row_index * n_col, n_col)
    spread_columns(next_dir[pl.ds(first, n_col), :], spread_v)
    row_acc[...] = jnp.zeros_like(row_acc)
    col_acc[...] = jnp.zeros_like(col_acc)

    fetch.wait()

    def step(turn, carry):
        for g in range(GROUP):
            slot = turn * GROUP + g
            j = pairs[slot, 1] * n_col + col_index
            add_tile(
                held[slot], slot, spread_v[pairs[slot, 0]], next_dir[pl.ds(j, 1), :],
                row_acc, col_acc,
                (row_index, col_index), pairs, listed, n_col,
            )
        return carry

    lax.fori_loop(0, pairs.shape[0] // GROUP, step, 0)
    write_slots(row_acc, col_acc, row_index, col_index, n_row, n_col, sums)
    partial = jnp.sum(sums[...] * next_dir[...])
    out_ref[:, 0:LANES] = sums[...]
    out_ref[:, LANES : 2 * LANES] = jnp.full((n_row * n_col, LANES), partial, jnp.float32)
    mine = pl.ds(row_index * n_col + col_index, 1)
    own_start = start_ref[mine, :]
    own_dir = next_dir[mine, :]
    own_ref[0:1, :] = alpha * own_start
    own_ref[1:2, :] = own_start - alpha * image_ref[mine, :]
    own_ref[2:3, :] = own_dir
    own_ref[3:4, :] = jnp.full((1, LANES), norm_1, jnp.float32)
    own_ref[4:5, :] = jnp.full((1, LANES), jnp.sum(direction * direction), jnp.float32)
    own_ref[5:8, :] = jnp.zeros((3, LANES), jnp.float32)


def image_kernel(place, partial_ref, own_ref, out_ref, *, block):
    total = jnp.sum(partial_ref[...], axis=0, keepdims=True)
    image = RIDGE * own_ref[...] + total * (1.0 / block)
    both = jnp.concatenate([image, own_ref[...]], axis=1)
    out_ref[...] = jnp.broadcast_to(both, out_ref.shape)


def finish_kernel(partial_ref, own_ref, solution_ref, residual_ref, *, block):
    total = jnp.sum(partial_ref[...], axis=0, keepdims=True)
    direction = own_ref[2:3, :]
    image = RIDGE * direction + total[:, 0:LANES] * (1.0 / block)
    against = RIDGE * own_ref[4:5, :] + total[:, LANES : 2 * LANES] * (1.0 / block)
    alpha = own_ref[3:4, :] / against
    solution_ref[...] = own_ref[0:1, :] + alpha * direction
    residual_ref[...] = own_ref[1:2, :] - alpha * image


def swap(slots):
    return lax.all_to_all(slots, AXES, 0, 0, tiled=True)


VM = pl.BlockSpec(memory_space=pltpu.VMEM)
SM = pl.BlockSpec(memory_space=pltpu.SMEM)
HB = pl.BlockSpec(memory_space=pltpu.HBM)
NX, NZ = 4, 4
NY, NH, NK = 4, 2, 2


def coords(device):
    row, col = divmod(device, NX * NZ)
    return row // 4, row // 2 % 2, row % 2, col // NZ, col % NZ


def device_at(y, half, core, x, z):
    return ((y % NY * NH + half) * NK + core) * NX * NZ + x % NX * NZ + z


def send(array, move):
    pairs = [(d, device_at(*move(*coords(d)))) for d in range(NY * NH * NK * NX * NZ)]
    return lax.ppermute(array, AXES, pairs)


def along_z(array, bit, only=range(NZ)):
    pairs = []
    for d in range(NY * NH * NK * NX * NZ):
        y, h, k, x, z = coords(d)
        if z in only:
            pairs.append((d, device_at(y, h, k, x, z ^ bit)))
    return lax.ppermute(array, AXES, pairs)


def along_x(array, step):
    return send(array, lambda y, h, k, x, z: (y, h, k, x + (step if k == 0 else -step), z))


def along_y(array, step):
    return send(array, lambda y, h, k, x, z: (y + (step if k == 0 else -step), h, k, x, z))


def across(array):
    return send(array, lambda y, h, k, x, z: (y, 1 - h, k, x, z))


def sibling(array):
    return send(array, lambda y, h, k, x, z: (y, h, 1 - k, x, z))


def together(*arrays):
    return lax.optimization_barrier(arrays[::-1])[::-1]


def gather(mine):
    z = lax.axis_index("col") % NZ
    middle = (z == 1) | (z == 2)
    inside = (1, 2)
    half = mine.shape[0] // 2

    one, two = along_x(mine, 1), along_x(mine, -1)
    z1, inner = along_z(mine, 1), along_z(mine, 3, inside)
    over_low = across(mine[:half])
    one, two, z1, inner, over_low = together(one, two, z1, inner, over_low)

    one1, two1, far = along_x(z1, 1), along_x(z1, -1), along_x(one, 1)
    over_high = across(mine[half:])
    inner2, outer = along_z(z1, 3, inside), along_z(inner, 1, inside)
    one1, two1, far, over_high, inner2, outer = together(
        one1, two1, far, over_high, inner2, outer
    )

    pair = jnp.stack([mine, jnp.concatenate([over_low, over_high])])
    z2 = jnp.where(middle, inner, outer)
    one2, two2, far1 = along_x(z2, 1), along_x(z2, -1), along_x(one1, 1)
    near, back = along_y(pair, 1), along_y(pair, -1)
    outer2 = along_z(inner2, 1, inside)
    one2, two2, far1, near, back, outer2 = together(one2, two2, far1, near, back, outer2)

    z3 = jnp.where(middle, inner2, outer2)
    one3, two3, far2 = along_x(z3, 1), along_x(z3, -1), along_x(one2, 1)
    rim = along_y(near, 1)
    twin = sibling(jnp.concatenate([pair, near, back]))
    one3, two3, far2, rim, twin = together(one3, two3, far2, rim, twin)

    far3, rim_twin = together(along_x(one3, 1), sibling(rim))

    rows = [mine, one, far, two, z1, one1, far1, two1, z2, one2, far2, two2, z3, one3, far3, two3]
    row_plan = [((NZ * turn + m, None),) for m in range(NZ) for turn in range(NX)]
    cols = [pair, near, rim, back, twin, rim_twin]
    col_plan = [((turn, 0), (4 + turn, 1)) for turn in range(NY)]
    col_plan += [
        ((8, 0), (12, 1), (9, 2), (13, 3), (11, 4), (15, 5)), ((10, 0), (14, 1)),
    ]
    return rows, row_plan, cols, col_plan


def spots():
    total = NY * NH * NK * NX * NZ
    row_spot = np.zeros((total, NX * NZ), np.int32)
    col_spot = np.zeros((total, NY * NH * NK), np.int32)
    for d in range(total):
        y, h, k, x, z = coords(d)
        sign = 1 if k == 0 else -1
        order = [z, z ^ 1, z ^ 3, z ^ 2] if z in (1, 2) else [z, z ^ 1, z ^ 2, z ^ 3]
        for a in range(NX * NZ):
            turn = sign * (x - a // NZ) % NX
            row_spot[d, a] = NZ * turn + order.index(a % NZ)
        for b in range(NY * NH * NK):
            swap_k = (b ^ k) & 1
            turn = (-sign if swap_k else sign) * (y - b // 4) % NY
            col_spot[d, b] = 8 * swap_k + 4 * ((b // 2 ^ h) & 1) + turn
    here = lax.axis_index("row") * NX * NZ + lax.axis_index("col")
    return jnp.asarray(row_spot)[here], jnp.asarray(col_spot)[here]


def body(features, targets, tile_pairs, tile_count):
    n_row = lax.axis_size("row")
    n_col = lax.axis_size("col")
    total = n_row * n_col
    place = jnp.stack([lax.axis_index("row"), lax.axis_index("col")]).astype(jnp.int32)
    pairs = tile_pairs[0, 0]
    count = tile_count[0]
    slots = pairs.shape[0]
    block, width = features.shape
    params = pltpu.CompilerParams(vmem_limit_bytes=SMALL)
    f32 = jnp.float32

    packed = pl.pallas_call(
        pack_kernel,
        out_shape=jax.ShapeDtypeStruct((block, width + LANES), jnp.bfloat16),
        in_specs=[VM, VM],
        out_specs=VM,
        compiler_params=params,
    )(features, targets[None, :])
    row_pieces, row_plan, col_pieces, col_plan = gather(packed)
    row_spot, col_spot = spots()

    accumulators = [
        pltpu.VMEM((n_col, block, block), f32),
        pltpu.VMEM((n_row, 8, block), f32),
    ]
    kernel, partial = pl.pallas_call(
        lambda *refs: first_sweep_kernel(row_plan, col_plan, width, *refs),
        out_shape=(
            jax.ShapeDtypeStruct((slots, block, block), f32),
            jax.ShapeDtypeStruct((total, block), f32),
        ),
        in_specs=[SM, SM, SM, SM, SM] + [HB] * (len(row_plan) + len(col_plan)),
        out_specs=(HB, VM),
        scratch_shapes=[
            pltpu.VMEM((slots, block, block), f32),
            pltpu.SemaphoreType.DMA((1,)),
            pltpu.VMEM((n_col, block, width + LANES), jnp.bfloat16),
            pltpu.VMEM((n_row, block, width + LANES), jnp.bfloat16),
        ]
        + [pltpu.SemaphoreType.DMA((sum(len(taken) for taken in row_plan + col_plan),))]
        + [pltpu.VMEM((n_row, block), f32)] * 2
        + [pltpu.VMEM((n_col, block, block), f32)] * 2 + accumulators,
        compiler_params=pltpu.CompilerParams(vmem_limit_bytes=LARGE),
    )(place, pairs, count, row_spot, col_spot, *row_pieces, *col_pieces)

    image = pl.pallas_call(
        lambda *refs: image_kernel(None, *refs, block=block),
        out_shape=jax.ShapeDtypeStruct((total, 2 * block), f32),
        in_specs=[VM, VM],
        out_specs=VM,
        compiler_params=params,
    )(swap(partial), targets[None, :])
    images = swap(image)

    partial_2, own = pl.pallas_call(
        lambda *refs: second_sweep_kernel(*refs, n_row=n_row, n_col=n_col),
        out_shape=(
            jax.ShapeDtypeStruct((total, 2 * block), f32),
            jax.ShapeDtypeStruct((8, block), f32),
        ),
        in_specs=[SM, SM, SM, HB, VM],
        out_specs=(VM, VM),
        scratch_shapes=[
            pltpu.VMEM((slots, block, block), f32),
            pltpu.SemaphoreType.DMA((1,)),
            pltpu.VMEM((total, block), f32),
            pltpu.VMEM((total, block), f32),
            pltpu.VMEM((total, block), f32),
            pltpu.VMEM((total, block), f32),
            pltpu.VMEM((n_col, block, block), f32),
        ] + accumulators,
        compiler_params=params,
    )(place, pairs, count, kernel, images)

    result, residual = pl.pallas_call(
        lambda *refs: finish_kernel(*refs, block=block),
        out_shape=(jax.ShapeDtypeStruct((1, block), f32),) * 2,
        in_specs=[VM, VM],
        out_specs=(VM, VM),
        compiler_params=params,
    )(swap(partial_2), own)
    return (result[0], residual[0])


def solution(mesh):
    return jax.shard_map(
        body,
        mesh=mesh,
        in_specs=(
            P(("row", "col"), None),
            P(("row", "col")),
            P("row", "col", None, None),
            P("row", "col"),
        ),
        out_specs=(P(("row", "col")), P(("row", "col"))),
        check_vma=False,
    )
```

```python
import jax
import jax.numpy as jnp
import numpy as np
from jax import lax
from jax.experimental import pallas as pl
from jax.experimental.pallas import tpu as pltpu
from jax.sharding import PartitionSpec as P

RIDGE = 1.0
GROUP = 4
STAGES = 4
AXES = ("row", "col")
LANES = 128
LARGE = 58 * 1024 * 1024
SMALL = 8 * 1024 * 1024


def spread_columns(values, out_ref):
    turned = jnp.transpose(values)
    for k in range(values.shape[0]):
        out_ref[k] = jnp.broadcast_to(turned[:, k : k + 1], (LANES, LANES))


def write_slots(row_acc, col_acc, row_index, col_index, n_row, n_col, out_ref):
    out_ref[...] = jnp.zeros_like(out_ref)
    lane = lax.broadcasted_iota(jnp.int32, (LANES, LANES), 1)
    packed = jnp.zeros((LANES, LANES), jnp.float32)
    for a in range(n_col):
        column = jnp.sum(row_acc[a], axis=1, keepdims=True)
        packed = packed + jnp.where(lane == a, column, 0.0)
    first = pl.multiple_of(row_index * n_col, n_col)
    out_ref[pl.ds(first, n_col), :] = jnp.transpose(packed)[0:n_col, :]
    for b in range(n_row):
        at = pl.ds(b * n_col + col_index, 1)
        out_ref[at, :] = out_ref[at, :] + jnp.sum(col_acc[b], axis=0, keepdims=True)


def split3(value):
    high = value.astype(jnp.bfloat16)
    rest = value - high.astype(jnp.float32)
    middle = rest.astype(jnp.bfloat16)
    return high, middle, (rest - middle.astype(jnp.float32)).astype(jnp.bfloat16)


def pack_kernel(features_ref, targets_ref, out_ref):
    width = features_ref.shape[1]
    wide = features_ref[...].astype(jnp.float32)
    norm = jnp.broadcast_to(jnp.sum(wide * wide, axis=1, keepdims=True), (LANES, LANES))
    target = jnp.transpose(jnp.broadcast_to(targets_ref[...], (LANES, LANES)))
    lane = lax.broadcasted_iota(jnp.int32, (LANES, LANES), 1)
    extra = jnp.zeros((LANES, LANES), jnp.float32)
    for k, part in enumerate(split3(target) + split3(norm)):
        extra = jnp.where(lane == k, part.astype(jnp.float32), extra)
    out_ref[:, 0:width] = features_ref[...]
    out_ref[:, width : width + LANES] = extra.astype(jnp.bfloat16)


def add_tile(kernel, slot, spread, across, row_acc, col_acc, where, tiles, n_col):
    row_index, col_index = where
    a = tiles[slot, 0]
    b = tiles[slot, 1]
    live = tiles[slot, 2].astype(jnp.float32)
    other = jnp.where(row_index * n_col + a == b * n_col + col_index, 0.0, live)
    both = kernel * (spread + across)
    row_acc[a] = row_acc[a] + both * live
    col_acc[b] = col_acc[b] + jnp.sum(both.reshape(16, 8, LANES), axis=0) * other


def first_sweep_kernel(
    row_plan, col_plan, width, place, tiles, ready, row_spot, col_spot, *rest
):
    n_pieces = len(row_plan) + len(col_plan)
    pieces = rest[:n_pieces]
    (kernel_ref, out_ref, held, held_sems, rows_ref, cols_ref, row_sems, col_sems, vec, norms,
     spread_v, spread_n, row_acc, col_acc) = rest[n_pieces:]
    n_col = rows_ref.shape[0]
    n_row = cols_ref.shape[0]
    copies = [[] for _ in range(STAGES)]
    for k, taken in enumerate(row_plan + col_plan):
        target, sems = (rows_ref, row_sems) if k < len(row_plan) else (cols_ref, col_sems)
        for index, part in taken:
            source = pieces[k] if part is None else pieces[k].at[part]
            copy = pltpu.make_async_copy(source, target.at[index], sems.at[index])
            copies[index * STAGES // n_col].append(copy)
    for copy in copies[0] + copies[1]:
        copy.start()
    row_index = place[0]
    col_index = place[1]
    row_acc[...] = jnp.zeros_like(row_acc)
    col_acc[...] = jnp.zeros_like(col_acc)

    lane = lax.broadcasted_iota(jnp.int32, (LANES, LANES), 0)
    take_v = (lane < 3).astype(jnp.float32).astype(jnp.bfloat16)
    take_n = ((lane >= 3) & (lane < 6)).astype(jnp.float32).astype(jnp.bfloat16)
    lane = lax.broadcasted_iota(jnp.int32, (16, LANES), 1)
    line = lax.broadcasted_iota(jnp.int32, (16, LANES), 0)
    take_both = (lane // 3 == line).astype(jnp.float32).astype(jnp.bfloat16)

    def spread(k):
        extra = rows_ref[k, :, width : width + LANES]
        spread_v[k] = jnp.dot(extra, take_v, preferred_element_type=jnp.float32)
        spread_n[k] = jnp.dot(extra, take_n, preferred_element_type=jnp.float32)
        both = lax.dot_general(
            take_both, cols_ref[k, :, width : width + LANES], (((1,), (1,)), ((), ())),
            preferred_element_type=jnp.float32,
        )
        vec[k : k + 1, :] = both[0:1, :]
        norms[k : k + 1, :] = both[1:2, :]

    def save(turn):
        at = pl.ds(turn * GROUP, GROUP)
        return pltpu.make_async_copy(held.at[at], kernel_ref.at[at], held_sems.at[turn])

    def step(turn, carry):
        for g in range(GROUP):
            slot = turn * GROUP + g
            a = row_spot[tiles[slot, 0]]
            b = col_spot[tiles[slot, 1]]
            inner = lax.dot_general(
                rows_ref[a, :, 0:width], cols_ref[b, :, 0:width], (((1,), (1,)), ((), ())),
                preferred_element_type=jnp.float32,
            )
            distance = spread_n[a] + norms[pl.ds(b, 1), :] - 2.0 * inner
            kernel = jnp.exp(jnp.maximum(distance, 0.0) * (-1.0 / width))
            held[slot] = kernel
            add_tile(
                kernel, slot, spread_v[a], vec[pl.ds(b, 1), :], row_acc, col_acc,
                (row_index, col_index), tiles, n_col,
            )
        save(turn).start()
        return carry

    turns = tiles.shape[0] // GROUP
    done = 0
    for stage in range(STAGES):
        for copy in copies[stage]:
            copy.wait()
        if stage + 2 < STAGES:
            for copy in copies[stage + 2]:
                copy.start()
        for k in range(n_col * stage // STAGES, n_col * (stage + 1) // STAGES):
            spread(k)
        upto = ready[stage] if stage + 1 < STAGES else turns
        lax.fori_loop(done, upto, step, 0)
        done = upto
    write_slots(row_acc, col_acc, row_index, col_index, n_row, n_col, out_ref)
    for turn in range(turns):
        save(turn).wait()


def second_sweep_kernel(
    place, tiles, kernel_ref, known_ref, out_ref, own_ref,
    held, held_sems, start_ref, image_ref, next_dir, sums, spread_v, row_acc, col_acc,
    *, n_row, n_col,
):
    fetch = pltpu.make_async_copy(kernel_ref, held, held_sems.at[0])
    fetch.start()
    row_index = place[0]
    col_index = place[1]
    image = known_ref[:, 0:LANES]
    start = known_ref[:, LANES : 2 * LANES]
    image_ref[...] = image
    start_ref[...] = start
    norm_0 = jnp.sum(start * start)
    alpha = norm_0 / jnp.sum(start * image)
    residual = start - alpha * image
    norm_1 = jnp.sum(residual * residual)
    direction = residual + (norm_1 / norm_0) * start
    next_dir[...] = direction
    first = pl.multiple_of(row_index * n_col, n_col)
    spread_columns(next_dir[pl.ds(first, n_col), :], spread_v)
    row_acc[...] = jnp.zeros_like(row_acc)
    col_acc[...] = jnp.zeros_like(col_acc)

    fetch.wait()

    def step(turn, carry):
        for g in range(GROUP):
            slot = turn * GROUP + g
            j = tiles[slot, 1] * n_col + col_index
            add_tile(
                held[slot], slot, spread_v[tiles[slot, 0]], next_dir[pl.ds(j, 1), :],
                row_acc, col_acc,
                (row_index, col_index), tiles, n_col,
            )
        return carry

    lax.fori_loop(0, tiles.shape[0] // GROUP, step, 0)
    write_slots(row_acc, col_acc, row_index, col_index, n_row, n_col, sums)
    partial = jnp.sum(sums[...] * next_dir[...])
    out_ref[:, 0:LANES] = sums[...]
    out_ref[:, LANES : 2 * LANES] = jnp.full((n_row * n_col, LANES), partial, jnp.float32)
    mine = pl.ds(row_index * n_col + col_index, 1)
    own_start = start_ref[mine, :]
    own_dir = next_dir[mine, :]
    own_ref[0:1, :] = alpha * own_start
    own_ref[1:2, :] = own_start - alpha * image_ref[mine, :]
    own_ref[2:3, :] = own_dir
    own_ref[3:4, :] = jnp.full((1, LANES), norm_1, jnp.float32)
    own_ref[4:5, :] = jnp.full((1, LANES), jnp.sum(direction * direction), jnp.float32)
    own_ref[5:8, :] = jnp.zeros((3, LANES), jnp.float32)


def image_kernel(place, partial_ref, own_ref, out_ref, *, block):
    total = jnp.sum(partial_ref[...], axis=0, keepdims=True)
    image = RIDGE * own_ref[...] + total * (1.0 / block)
    both = jnp.concatenate([image, own_ref[...]], axis=1)
    out_ref[...] = jnp.broadcast_to(both, out_ref.shape)


def finish_kernel(partial_ref, own_ref, solution_ref, residual_ref, *, block):
    total = jnp.sum(partial_ref[...], axis=0, keepdims=True)
    direction = own_ref[2:3, :]
    image = RIDGE * direction + total[:, 0:LANES] * (1.0 / block)
    against = RIDGE * own_ref[4:5, :] + total[:, LANES : 2 * LANES] * (1.0 / block)
    alpha = own_ref[3:4, :] / against
    solution_ref[...] = own_ref[0:1, :] + alpha * direction
    residual_ref[...] = own_ref[1:2, :] - alpha * image


def in_order(pairs, count, row_spot, col_spot):
    slots = pairs.shape[0]
    spots_of = jnp.arange(row_spot.shape[0], dtype=jnp.int32)[None, :]
    row_at = jnp.sum(jnp.where(pairs[:, 0:1] == spots_of, row_spot[None, :], 0), axis=1)
    col_at = jnp.sum(jnp.where(pairs[:, 1:2] == spots_of, col_spot[None, :], 0), axis=1)
    slot = jnp.arange(slots, dtype=jnp.int32)
    arrival = jnp.maximum(row_at, col_at)
    key = arrival * slots + slot
    rank = jnp.sum((key[None, :] < key[:, None]).astype(jnp.int32), axis=1)
    known = jnp.stack([pairs[:, 0], pairs[:, 1], (slot < count).astype(jnp.int32)], axis=1)
    chosen = rank[None, :] == slot[:, None]
    tiles = jnp.sum(jnp.where(chosen[:, :, None], known[None, :, :], 0), axis=1)
    fetched = (jnp.arange(STAGES, dtype=jnp.int32) + 1) * (row_spot.shape[0] // STAGES)
    ready = jnp.sum((arrival[None, :] < fetched[:, None]).astype(jnp.int32), axis=1) // GROUP
    return tiles, ready


def swap(slots):
    return lax.all_to_all(slots, AXES, 0, 0, tiled=True)


VM = pl.BlockSpec(memory_space=pltpu.VMEM)
SM = pl.BlockSpec(memory_space=pltpu.SMEM)
HB = pl.BlockSpec(memory_space=pltpu.HBM)
NX, NZ = 4, 4
NY, NH, NK = 4, 2, 2


def coords(device):
    row, col = divmod(device, NX * NZ)
    return row // 4, row // 2 % 2, row % 2, col // NZ, col % NZ


def device_at(y, half, core, x, z):
    return ((y % NY * NH + half) * NK + core) * NX * NZ + x % NX * NZ + z


def send(array, move):
    pairs = [(d, device_at(*move(*coords(d)))) for d in range(NY * NH * NK * NX * NZ)]
    return lax.ppermute(array, AXES, pairs)


def along_z(array, bit, only=range(NZ)):
    pairs = []
    for d in range(NY * NH * NK * NX * NZ):
        y, h, k, x, z = coords(d)
        if z in only:
            pairs.append((d, device_at(y, h, k, x, z ^ bit)))
    return lax.ppermute(array, AXES, pairs)


def along_x(array, step):
    return send(array, lambda y, h, k, x, z: (y, h, k, x + (step if k == 0 else -step), z))


def along_y(array, step):
    return send(array, lambda y, h, k, x, z: (y + (step if k == 0 else -step), h, k, x, z))


def across(array):
    return send(array, lambda y, h, k, x, z: (y, 1 - h, k, x, z))


def sibling(array):
    return send(array, lambda y, h, k, x, z: (y, h, 1 - k, x, z))


def together(*arrays):
    return lax.optimization_barrier(arrays[::-1])[::-1]


def gather(mine):
    z = lax.axis_index("col") % NZ
    middle = (z == 1) | (z == 2)
    inside = (1, 2)

    z3, z1 = along_z(mine, 3), along_z(mine, 1)
    one, two = along_x(mine, 1), along_x(mine, -1)
    near, back = along_y(mine, 1), along_y(mine, -1)
    z3, z1, one, two, near, back = together(z3, z1, one, two, near, back)

    over = across(mine)
    z13 = jnp.stack([z1, z3])
    one13, two13 = along_x(z13, 1), along_x(z13, -1)
    inner, outer = along_z(z1, 3, inside), along_z(z3, 1, inside)
    far, rim = along_x(one, 1), along_y(near, 1)
    over, one13, two13, inner, outer, far, rim = together(
        over, one13, two13, inner, outer, far, rim
    )

    z2 = jnp.where(middle, inner, outer)
    far13, one2, two2 = along_x(one13, 1), along_x(z2, 1), along_x(z2, -1)
    near_c, back_c = along_y(over, 1), along_y(over, -1)
    line = jnp.stack([mine, near, rim, back])
    far13, one2, two2, near_c, back_c, line = together(far13, one2, two2, near_c, back_c, line)

    far2, rim_c = along_x(one2, 1), along_y(near_c, 1)
    twin, twin_c = sibling(line), sibling(jnp.stack([over, near_c, back_c]))
    rim_c, far2, twin, twin_c = together(rim_c, far2, twin, twin_c)

    rim_twin = sibling(rim_c)

    rows = [mine, one, far, two, z13, one13, far13, two13, z2, one2, far2, two2]
    row_plan = [((NZ * turn, None),) for turn in range(NX)]
    row_plan += [((NZ * turn + 1, 0), (NZ * turn + 2, 1)) for turn in range(NX)]
    row_plan += [((NZ * turn + 3, None),) for turn in range(NX)]
    cols = [line, over, near_c, rim_c, back_c, twin, twin_c, rim_twin]
    col_plan = [tuple((k, k) for k in range(NY))] + [((k, None),) for k in range(NY, 2 * NY)]
    col_plan += [tuple((8 + k, k) for k in range(NY)), ((12, 0), (13, 1), (15, 2)), ((14, None),)]
    return rows, row_plan, cols, col_plan


def spots():
    total = NY * NH * NK * NX * NZ
    row_spot = np.zeros((total, NX * NZ), np.int32)
    col_spot = np.zeros((total, NY * NH * NK), np.int32)
    for d in range(total):
        y, h, k, x, z = coords(d)
        sign = 1 if k == 0 else -1
        order = [z, z ^ 1, z ^ 3, z ^ 2]
        for a in range(NX * NZ):
            turn = sign * (x - a // NZ) % NX
            row_spot[d, a] = NZ * turn + order.index(a % NZ)
        for b in range(NY * NH * NK):
            swap_k = (b ^ k) & 1
            turn = (-sign if swap_k else sign) * (y - b // 4) % NY
            col_spot[d, b] = 8 * swap_k + 4 * ((b // 2 ^ h) & 1) + turn
    here = lax.axis_index("row") * NX * NZ + lax.axis_index("col")
    return jnp.asarray(row_spot)[here], jnp.asarray(col_spot)[here]


def body(features, targets, tile_pairs, tile_count):
    n_row = lax.axis_size("row")
    n_col = lax.axis_size("col")
    total = n_row * n_col
    place = jnp.stack([lax.axis_index("row"), lax.axis_index("col")]).astype(jnp.int32)
    pairs = tile_pairs[0, 0]
    count = tile_count[0, 0]
    slots = pairs.shape[0]
    block, width = features.shape
    params = pltpu.CompilerParams(vmem_limit_bytes=SMALL)
    f32 = jnp.float32

    packed = pl.pallas_call(
        pack_kernel,
        out_shape=jax.ShapeDtypeStruct((block, width + LANES), jnp.bfloat16),
        in_specs=[VM, VM],
        out_specs=VM,
        compiler_params=params,
    )(features, targets[None, :])
    row_pieces, row_plan, col_pieces, col_plan = gather(packed)
    row_spot, col_spot = spots()
    tiles, ready = in_order(pairs, count, row_spot, col_spot)

    accumulators = [
        pltpu.VMEM((n_col, block, block), f32),
        pltpu.VMEM((n_row, 8, block), f32),
    ]
    kernel, partial = pl.pallas_call(
        lambda *refs: first_sweep_kernel(row_plan, col_plan, width, *refs),
        out_shape=(
            jax.ShapeDtypeStruct((slots, block, block), f32),
            jax.ShapeDtypeStruct((total, block), f32),
        ),
        in_specs=[SM, SM, SM, SM, SM] + [HB] * (len(row_plan) + len(col_plan)),
        out_specs=(HB, VM),
        scratch_shapes=[
            pltpu.VMEM((slots, block, block), f32),
            pltpu.SemaphoreType.DMA((slots // GROUP,)),
            pltpu.VMEM((n_col, block, width + LANES), jnp.bfloat16),
            pltpu.VMEM((n_row, block, width + LANES), jnp.bfloat16),
        ]
        + [pltpu.SemaphoreType.DMA((n_col,)), pltpu.SemaphoreType.DMA((n_row,))]
        + [pltpu.VMEM((n_row, block), f32)] * 2
        + [pltpu.VMEM((n_col, block, block), f32)] * 2 + accumulators,
        compiler_params=pltpu.CompilerParams(vmem_limit_bytes=LARGE),
    )(place, tiles, ready, row_spot, col_spot, *row_pieces, *col_pieces)

    image = pl.pallas_call(
        lambda *refs: image_kernel(None, *refs, block=block),
        out_shape=jax.ShapeDtypeStruct((total, 2 * block), f32),
        in_specs=[VM, VM],
        out_specs=VM,
        compiler_params=params,
    )(swap(partial), targets[None, :])
    images = swap(image)

    partial_2, own = pl.pallas_call(
        lambda *refs: second_sweep_kernel(*refs, n_row=n_row, n_col=n_col),
        out_shape=(
            jax.ShapeDtypeStruct((total, 2 * block), f32),
            jax.ShapeDtypeStruct((8, block), f32),
        ),
        in_specs=[SM, SM, HB, VM],
        out_specs=(VM, VM),
        scratch_shapes=[
            pltpu.VMEM((slots, block, block), f32),
            pltpu.SemaphoreType.DMA((1,)),
            pltpu.VMEM((total, block), f32),
            pltpu.VMEM((total, block), f32),
            pltpu.VMEM((total, block), f32),
            pltpu.VMEM((total, block), f32),
            pltpu.VMEM((n_col, block, block), f32),
        ] + accumulators,
        compiler_params=params,
    )(place, tiles, kernel, images)

    result, residual = pl.pallas_call(
        lambda *refs: finish_kernel(*refs, block=block),
        out_shape=(jax.ShapeDtypeStruct((1, block), f32),) * 2,
        in_specs=[VM, VM],
        out_specs=(VM, VM),
        compiler_params=params,
    )(swap(partial_2), own)
    return (result[0], residual[0])


def solution(mesh):
    return jax.shard_map(
        body,
        mesh=mesh,
        in_specs=(
            P(("row", "col"), None),
            P(("row", "col")),
            P("row", "col", None, None),
            P("row", "col"),
        ),
        out_specs=(P(("row", "col")), P(("row", "col"))),
        check_vma=False,
    )
```

```python
import jax
import jax.numpy as jnp
import numpy as np
from jax import lax
from jax.experimental import pallas as pl
from jax.experimental.pallas import tpu as pltpu
from jax.sharding import PartitionSpec as P

RIDGE = 1.0
GROUP = 4
STAGES = 4
AXES = ("row", "col")
LANES = 128
LARGE = 58 * 1024 * 1024
SMALL = 8 * 1024 * 1024


def spread_columns(values, out_ref):
    turned = jnp.transpose(values)
    for k in range(values.shape[0]):
        out_ref[k] = jnp.broadcast_to(turned[:, k : k + 1], (LANES, LANES))


def write_slots(row_acc, col_acc, row_index, col_index, n_row, n_col, out_ref):
    out_ref[...] = jnp.zeros_like(out_ref)
    lane = lax.broadcasted_iota(jnp.int32, (LANES, LANES), 1)
    packed = jnp.zeros((LANES, LANES), jnp.float32)
    for a in range(n_col):
        column = jnp.sum(row_acc[a], axis=1, keepdims=True)
        packed = packed + jnp.where(lane == a, column, 0.0)
    first = pl.multiple_of(row_index * n_col, n_col)
    out_ref[pl.ds(first, n_col), :] = jnp.transpose(packed)[0:n_col, :]
    for b in range(n_row):
        at = pl.ds(b * n_col + col_index, 1)
        out_ref[at, :] = out_ref[at, :] + jnp.sum(col_acc[b], axis=0, keepdims=True)


def split3(value):
    high = value.astype(jnp.bfloat16)
    rest = value - high.astype(jnp.float32)
    middle = rest.astype(jnp.bfloat16)
    return high, middle, (rest - middle.astype(jnp.float32)).astype(jnp.bfloat16)


def pack_kernel(features_ref, targets_ref, out_ref):
    width = features_ref.shape[1]
    wide = features_ref[...].astype(jnp.float32)
    norm = jnp.broadcast_to(jnp.sum(wide * wide, axis=1, keepdims=True), (LANES, LANES))
    target = jnp.transpose(jnp.broadcast_to(targets_ref[...], (LANES, LANES)))
    lane = lax.broadcasted_iota(jnp.int32, (LANES, LANES), 1)
    extra = jnp.zeros((LANES, LANES), jnp.float32)
    for k, part in enumerate(split3(target) + split3(norm)):
        extra = jnp.where(lane == k, part.astype(jnp.float32), extra)
    out_ref[:, 0:width] = features_ref[...]
    out_ref[:, width : width + LANES] = extra.astype(jnp.bfloat16)


def add_tile(kernel, slot, spread, across, row_acc, col_acc, where, tiles, n_col):
    row_index, col_index = where
    a = tiles[slot, 0]
    b = tiles[slot, 1]
    live = tiles[slot, 2].astype(jnp.float32)
    other = jnp.where(row_index * n_col + a == b * n_col + col_index, 0.0, live)
    both = kernel * (spread + across)
    row_acc[a] = row_acc[a] + both * live
    col_acc[b] = col_acc[b] + jnp.sum(both.reshape(16, 8, LANES), axis=0) * other


def first_sweep_kernel(
    row_plan, col_plan, width, place, tiles, ready, row_spot, col_spot, *rest
):
    n_pieces = len(row_plan) + len(col_plan)
    pieces = rest[:n_pieces]
    (kernel_ref, out_ref, held, held_sems, rows_ref, cols_ref, row_sems, col_sems, vec, norms,
     spread_v, spread_n, row_acc, col_acc) = rest[n_pieces:]
    n_col = rows_ref.shape[0]
    n_row = cols_ref.shape[0]
    copies = [[] for _ in range(STAGES)]
    for k, taken in enumerate(row_plan + col_plan):
        target, sems = (rows_ref, row_sems) if k < len(row_plan) else (cols_ref, col_sems)
        for index, part in taken:
            source = pieces[k] if part is None else pieces[k].at[part]
            copy = pltpu.make_async_copy(source, target.at[index], sems.at[index])
            copies[index * STAGES // n_col].append(copy)
    for copy in copies[0] + copies[1]:
        copy.start()
    row_index = place[0]
    col_index = place[1]
    row_acc[...] = jnp.zeros_like(row_acc)
    col_acc[...] = jnp.zeros_like(col_acc)

    lane = lax.broadcasted_iota(jnp.int32, (LANES, LANES), 0)
    take_v = (lane < 3).astype(jnp.float32).astype(jnp.bfloat16)
    take_n = ((lane >= 3) & (lane < 6)).astype(jnp.float32).astype(jnp.bfloat16)
    lane = lax.broadcasted_iota(jnp.int32, (16, LANES), 1)
    line = lax.broadcasted_iota(jnp.int32, (16, LANES), 0)
    take_both = (lane // 3 == line).astype(jnp.float32).astype(jnp.bfloat16)

    def spread(k):
        extra = rows_ref[k, :, width : width + LANES]
        spread_v[k] = jnp.dot(extra, take_v, preferred_element_type=jnp.float32)
        spread_n[k] = jnp.dot(extra, take_n, preferred_element_type=jnp.float32)
        both = lax.dot_general(
            take_both, cols_ref[k, :, width : width + LANES], (((1,), (1,)), ((), ())),
            preferred_element_type=jnp.float32,
        )
        vec[k : k + 1, :] = both[0:1, :]
        norms[k : k + 1, :] = both[1:2, :]

    def save(turn):
        at = pl.ds(turn * GROUP, GROUP)
        return pltpu.make_async_copy(held.at[at], kernel_ref.at[at], held_sems.at[turn])

    def step(turn, carry):
        for g in range(GROUP):
            slot = turn * GROUP + g
            a = row_spot[tiles[slot, 0]]
            b = col_spot[tiles[slot, 1]]
            inner = lax.dot_general(
                rows_ref[a, :, 0:width], cols_ref[b, :, 0:width], (((1,), (1,)), ((), ())),
                preferred_element_type=jnp.float32,
            )
            distance = spread_n[a] + norms[pl.ds(b, 1), :] - 2.0 * inner
            kernel = jnp.exp(jnp.maximum(distance, 0.0) * (-1.0 / width))
            held[slot] = kernel
            add_tile(
                kernel, slot, spread_v[a], vec[pl.ds(b, 1), :], row_acc, col_acc,
                (row_index, col_index), tiles, n_col,
            )
        save(turn).start()
        return carry

    turns = tiles.shape[0] // GROUP
    done = 0
    for stage in range(STAGES):
        for copy in copies[stage]:
            copy.wait()
        if stage + 2 < STAGES:
            for copy in copies[stage + 2]:
                copy.start()
        for k in range(n_col * stage // STAGES, n_col * (stage + 1) // STAGES):
            spread(k)
        upto = ready[stage] if stage + 1 < STAGES else turns
        lax.fori_loop(done, upto, step, 0)
        done = upto
    write_slots(row_acc, col_acc, row_index, col_index, n_row, n_col, out_ref)
    for turn in range(turns):
        save(turn).wait()


def second_sweep_kernel(
    place, tiles, kernel_ref, known_ref, out_ref, own_ref,
    held, held_sems, start_ref, image_ref, next_dir, sums, spread_v, row_acc, col_acc,
    *, n_row, n_col,
):
    fetch = pltpu.make_async_copy(kernel_ref, held, held_sems.at[0])
    fetch.start()
    row_index = place[0]
    col_index = place[1]
    image = known_ref[:, 0:LANES]
    start = known_ref[:, LANES : 2 * LANES]
    image_ref[...] = image
    start_ref[...] = start
    norm_0 = jnp.sum(start * start)
    alpha = norm_0 / jnp.sum(start * image)
    residual = start - alpha * image
    norm_1 = jnp.sum(residual * residual)
    direction = residual + (norm_1 / norm_0) * start
    next_dir[...] = direction
    first = pl.multiple_of(row_index * n_col, n_col)
    spread_columns(next_dir[pl.ds(first, n_col), :], spread_v)
    row_acc[...] = jnp.zeros_like(row_acc)
    col_acc[...] = jnp.zeros_like(col_acc)

    fetch.wait()

    def step(turn, carry):
        for g in range(GROUP):
            slot = turn * GROUP + g
            j = tiles[slot, 1] * n_col + col_index
            add_tile(
                held[slot], slot, spread_v[tiles[slot, 0]], next_dir[pl.ds(j, 1), :],
                row_acc, col_acc,
                (row_index, col_index), tiles, n_col,
            )
        return carry

    lax.fori_loop(0, tiles.shape[0] // GROUP, step, 0)
    write_slots(row_acc, col_acc, row_index, col_index, n_row, n_col, sums)
    partial = jnp.sum(sums[...] * next_dir[...])
    out_ref[:, 0:LANES] = sums[...]
    out_ref[:, LANES : 2 * LANES] = jnp.full((n_row * n_col, LANES), partial, jnp.float32)
    mine = pl.ds(row_index * n_col + col_index, 1)
    own_start = start_ref[mine, :]
    own_dir = next_dir[mine, :]
    own_ref[0:1, :] = alpha * own_start
    own_ref[1:2, :] = own_start - alpha * image_ref[mine, :]
    own_ref[2:3, :] = own_dir
    own_ref[3:4, :] = jnp.full((1, LANES), norm_1, jnp.float32)
    own_ref[4:5, :] = jnp.full((1, LANES), jnp.sum(direction * direction), jnp.float32)
    own_ref[5:8, :] = jnp.zeros((3, LANES), jnp.float32)


def image_kernel(place, partial_ref, own_ref, out_ref, *, block):
    total = jnp.sum(partial_ref[...], axis=0, keepdims=True)
    image = RIDGE * own_ref[...] + total * (1.0 / block)
    both = jnp.concatenate([image, own_ref[...]], axis=1)
    out_ref[...] = jnp.broadcast_to(both, out_ref.shape)


def finish_kernel(partial_ref, own_ref, solution_ref, residual_ref, *, block):
    total = jnp.sum(partial_ref[...], axis=0, keepdims=True)
    direction = own_ref[2:3, :]
    image = RIDGE * direction + total[:, 0:LANES] * (1.0 / block)
    against = RIDGE * own_ref[4:5, :] + total[:, LANES : 2 * LANES] * (1.0 / block)
    alpha = own_ref[3:4, :] / against
    solution_ref[...] = own_ref[0:1, :] + alpha * direction
    residual_ref[...] = own_ref[1:2, :] - alpha * image


def in_order(pairs, count, row_spot, col_spot):
    slots = pairs.shape[0]
    spots_of = jnp.arange(row_spot.shape[0], dtype=jnp.int32)[None, :]
    row_at = jnp.sum(jnp.where(pairs[:, 0:1] == spots_of, row_spot[None, :], 0), axis=1)
    col_at = jnp.sum(jnp.where(pairs[:, 1:2] == spots_of, col_spot[None, :], 0), axis=1)
    slot = jnp.arange(slots, dtype=jnp.int32)
    arrival = jnp.maximum(row_at, col_at)
    key = arrival * slots + slot
    rank = jnp.sum((key[None, :] < key[:, None]).astype(jnp.int32), axis=1)
    known = jnp.stack([pairs[:, 0], pairs[:, 1], (slot < count).astype(jnp.int32)], axis=1)
    chosen = rank[None, :] == slot[:, None]
    tiles = jnp.sum(jnp.where(chosen[:, :, None], known[None, :, :], 0), axis=1)
    fetched = (jnp.arange(STAGES, dtype=jnp.int32) + 1) * (row_spot.shape[0] // STAGES)
    ready = jnp.sum((arrival[None, :] < fetched[:, None]).astype(jnp.int32), axis=1) // GROUP
    return tiles, ready


def swap(slots):
    return lax.all_to_all(slots, AXES, 0, 0, tiled=True)


VM = pl.BlockSpec(memory_space=pltpu.VMEM)
SM = pl.BlockSpec(memory_space=pltpu.SMEM)
HB = pl.BlockSpec(memory_space=pltpu.HBM)
NX, NZ = 4, 4
NY, NH, NK = 4, 2, 2


def coords(device):
    row, col = divmod(device, NX * NZ)
    return row // 4, row // 2 % 2, row % 2, col // NZ, col % NZ


def device_at(y, half, core, x, z):
    return ((y % NY * NH + half) * NK + core) * NX * NZ + x % NX * NZ + z


def send(array, move):
    pairs = [(d, device_at(*move(*coords(d)))) for d in range(NY * NH * NK * NX * NZ)]
    return lax.ppermute(array, AXES, pairs)


def along_z(array, bit, only=range(NZ)):
    pairs = []
    for d in range(NY * NH * NK * NX * NZ):
        y, h, k, x, z = coords(d)
        if z in only:
            pairs.append((d, device_at(y, h, k, x, z ^ bit)))
    return lax.ppermute(array, AXES, pairs)


def along_x(array, step):
    return send(array, lambda y, h, k, x, z: (y, h, k, x + (step if k == 0 else -step), z))


def along_y(array, step):
    return send(array, lambda y, h, k, x, z: (y + (step if k == 0 else -step), h, k, x, z))


def across(array):
    return send(array, lambda y, h, k, x, z: (y, 1 - h, k, x, z))


def sibling(array):
    return send(array, lambda y, h, k, x, z: (y, h, 1 - k, x, z))


def together(*arrays):
    return lax.optimization_barrier(arrays[::-1])[::-1]


def gather(mine, small):
    z = lax.axis_index("col") % NZ
    middle = (z == 1) | (z == 2)
    inside = (1, 2)

    z3, z1 = along_z(mine, 3), along_z(mine, 1)
    one, two = along_x(mine, 1), along_x(mine, -1)
    near, back = along_y(mine, 1), along_y(mine, -1)
    z3, z1, one, two, near, back = together(z3, z1, one, two, near, back)

    over = across(mine)
    z13 = jnp.stack([z1, z3])
    one13, two13 = along_x(z13, 1), along_x(z13, -1)
    inner, outer = along_z(z1, 3, inside), along_z(z3, 1, inside)
    far, rim = along_x(one, 1), along_y(near, 1)
    over, one13, two13, inner, outer, far, rim = together(
        over, one13, two13, inner, outer, far, rim
    )

    z2 = jnp.where(middle, inner, outer)
    far13, one2, two2 = along_x(one13, 1), along_x(z2, 1), along_x(z2, -1)
    near_c, back_c = along_y(over, 1), along_y(over, -1)
    line = jnp.stack([mine, near, rim, back])
    far13, one2, two2, near_c, back_c, line, *small = together(
        far13, one2, two2, near_c, back_c, line, *small
    )

    far2, rim_c = along_x(one2, 1), along_y(near_c, 1)
    twin, twin_c = sibling(line), sibling(jnp.stack([over, near_c, back_c]))
    rim_c, far2, twin, twin_c = together(rim_c, far2, twin, twin_c)

    rim_twin = sibling(rim_c)

    rows = [mine, one, far, two, z13, one13, far13, two13, z2, one2, far2, two2]
    row_plan = [((NZ * turn, None),) for turn in range(NX)]
    row_plan += [((NZ * turn + 1, 0), (NZ * turn + 2, 1)) for turn in range(NX)]
    row_plan += [((NZ * turn + 3, None),) for turn in range(NX)]
    cols = [line, over, near_c, rim_c, back_c, twin, twin_c, rim_twin]
    col_plan = [tuple((k, k) for k in range(NY))] + [((k, None),) for k in range(NY, 2 * NY)]
    col_plan += [tuple((8 + k, k) for k in range(NY)), ((12, 0), (13, 1), (15, 2)), ((14, None),)]
    return rows, row_plan, cols, col_plan, small


def spots():
    total = NY * NH * NK * NX * NZ
    row_spot = np.zeros((total, NX * NZ), np.int32)
    col_spot = np.zeros((total, NY * NH * NK), np.int32)
    for d in range(total):
        y, h, k, x, z = coords(d)
        sign = 1 if k == 0 else -1
        order = [z, z ^ 1, z ^ 3, z ^ 2]
        for a in range(NX * NZ):
            turn = sign * (x - a // NZ) % NX
            row_spot[d, a] = NZ * turn + order.index(a % NZ)
        for b in range(NY * NH * NK):
            swap_k = (b ^ k) & 1
            turn = (-sign if swap_k else sign) * (y - b // 4) % NY
            col_spot[d, b] = 8 * swap_k + 4 * ((b // 2 ^ h) & 1) + turn
    here = lax.axis_index("row") * NX * NZ + lax.axis_index("col")
    return jnp.asarray(row_spot)[here], jnp.asarray(col_spot)[here]


def body(features, targets, tile_pairs, tile_count):
    n_row = lax.axis_size("row")
    n_col = lax.axis_size("col")
    total = n_row * n_col
    place = jnp.stack([lax.axis_index("row"), lax.axis_index("col")]).astype(jnp.int32)
    pairs = tile_pairs[0, 0]
    count = tile_count[0, 0]
    slots = pairs.shape[0]
    block, width = features.shape
    params = pltpu.CompilerParams(vmem_limit_bytes=SMALL)
    f32 = jnp.float32

    packed = pl.pallas_call(
        pack_kernel,
        out_shape=jax.ShapeDtypeStruct((block, width + LANES), jnp.bfloat16),
        in_specs=[VM, VM],
        out_specs=VM,
        compiler_params=params,
    )(features, targets[None, :])
    row_spot, col_spot = spots()
    tiles, ready = in_order(pairs, count, row_spot, col_spot)
    small = (place, tiles, ready, row_spot, col_spot)
    row_pieces, row_plan, col_pieces, col_plan, small = gather(packed, small)
    place, tiles, ready, row_spot, col_spot = small

    accumulators = [
        pltpu.VMEM((n_col, block, block), f32),
        pltpu.VMEM((n_row, 8, block), f32),
    ]
    kernel, partial = pl.pallas_call(
        lambda *refs: first_sweep_kernel(row_plan, col_plan, width, *refs),
        out_shape=(
            jax.ShapeDtypeStruct((slots, block, block), f32),
            jax.ShapeDtypeStruct((total, block), f32),
        ),
        in_specs=[SM, SM, SM, SM, SM] + [HB] * (len(row_plan) + len(col_plan)),
        out_specs=(HB, VM),
        scratch_shapes=[
            pltpu.VMEM((slots, block, block), f32),
            pltpu.SemaphoreType.DMA((slots // GROUP,)),
            pltpu.VMEM((n_col, block, width + LANES), jnp.bfloat16),
            pltpu.VMEM((n_row, block, width + LANES), jnp.bfloat16),
        ]
        + [pltpu.SemaphoreType.DMA((n_col,)), pltpu.SemaphoreType.DMA((n_row,))]
        + [pltpu.VMEM((n_row, block), f32)] * 2
        + [pltpu.VMEM((n_col, block, block), f32)] * 2 + accumulators,
        compiler_params=pltpu.CompilerParams(vmem_limit_bytes=LARGE),
    )(place, tiles, ready, row_spot, col_spot, *row_pieces, *col_pieces)

    image = pl.pallas_call(
        lambda *refs: image_kernel(None, *refs, block=block),
        out_shape=jax.ShapeDtypeStruct((total, 2 * block), f32),
        in_specs=[VM, VM],
        out_specs=VM,
        compiler_params=params,
    )(swap(partial), targets[None, :])
    images = swap(image)

    partial_2, own = pl.pallas_call(
        lambda *refs: second_sweep_kernel(*refs, n_row=n_row, n_col=n_col),
        out_shape=(
            jax.ShapeDtypeStruct((total, 2 * block), f32),
            jax.ShapeDtypeStruct((8, block), f32),
        ),
        in_specs=[SM, SM, HB, VM],
        out_specs=(VM, VM),
        scratch_shapes=[
            pltpu.VMEM((slots, block, block), f32),
            pltpu.SemaphoreType.DMA((1,)),
            pltpu.VMEM((total, block), f32),
            pltpu.VMEM((total, block), f32),
            pltpu.VMEM((total, block), f32),
            pltpu.VMEM((total, block), f32),
            pltpu.VMEM((n_col, block, block), f32),
        ] + accumulators,
        compiler_params=params,
    )(place, tiles, kernel, images)

    result, residual = pl.pallas_call(
        lambda *refs: finish_kernel(*refs, block=block),
        out_shape=(jax.ShapeDtypeStruct((1, block), f32),) * 2,
        in_specs=[VM, VM],
        out_specs=(VM, VM),
        compiler_params=params,
    )(swap(partial_2), own)
    return (result[0], residual[0])


def solution(mesh):
    return jax.shard_map(
        body,
        mesh=mesh,
        in_specs=(
            P(("row", "col"), None),
            P(("row", "col")),
            P("row", "col", None, None),
            P("row", "col"),
        ),
        out_specs=(P(("row", "col")), P(("row", "col"))),
        check_vma=False,
    )
```

```python
import jax
import jax.numpy as jnp
import numpy as np
from jax import lax
from jax.experimental import pallas as pl
from jax.experimental.pallas import tpu as pltpu
from jax.sharding import PartitionSpec as P

RIDGE = 1.0
GROUP = 8
STAGES = 4
AXES = ("row", "col")
LANES = 128
LARGE = 58 * 1024 * 1024
SMALL = 8 * 1024 * 1024


def spread_columns(values, out_ref):
    turned = jnp.transpose(values)
    for k in range(values.shape[0]):
        out_ref[k] = jnp.broadcast_to(turned[:, k : k + 1], (LANES, LANES))


def write_slots(row_acc, col_acc, row_index, col_index, n_row, n_col, out_ref):
    out_ref[...] = jnp.zeros_like(out_ref)
    lane = lax.broadcasted_iota(jnp.int32, (LANES, LANES), 1)
    packed = jnp.zeros((LANES, LANES), jnp.float32)
    for a in range(n_col):
        column = jnp.sum(row_acc[a], axis=1, keepdims=True)
        packed = packed + jnp.where(lane == a, column, 0.0)
    first = pl.multiple_of(row_index * n_col, n_col)
    out_ref[pl.ds(first, n_col), :] = jnp.transpose(packed)[0:n_col, :]
    for b in range(n_row):
        at = pl.ds(b * n_col + col_index, 1)
        out_ref[at, :] = out_ref[at, :] + jnp.sum(col_acc[b], axis=0, keepdims=True)


def split3(value):
    high = value.astype(jnp.bfloat16)
    rest = value - high.astype(jnp.float32)
    middle = rest.astype(jnp.bfloat16)
    return high, middle, (rest - middle.astype(jnp.float32)).astype(jnp.bfloat16)


def pack_kernel(features_ref, targets_ref, out_ref):
    width = features_ref.shape[1]
    wide = features_ref[...].astype(jnp.float32)
    norm = jnp.broadcast_to(jnp.sum(wide * wide, axis=1, keepdims=True), (LANES, LANES))
    target = jnp.transpose(jnp.broadcast_to(targets_ref[...], (LANES, LANES)))
    lane = lax.broadcasted_iota(jnp.int32, (LANES, LANES), 1)
    extra = jnp.zeros((LANES, LANES), jnp.float32)
    for k, part in enumerate(split3(target) + split3(norm)):
        extra = jnp.where(lane == k, part.astype(jnp.float32), extra)
    out_ref[:, 0:width] = features_ref[...]
    out_ref[:, width : width + LANES] = extra.astype(jnp.bfloat16)


def add_tile(kernel, slot, spread, across, row_acc, col_acc, where, tiles, n_col):
    row_index, col_index = where
    a = tiles[slot, 0]
    b = tiles[slot, 1]
    live = tiles[slot, 2].astype(jnp.float32)
    other = jnp.where(row_index * n_col + a == b * n_col + col_index, 0.0, live)
    both = kernel * (spread + across)
    row_acc[a] = row_acc[a] + both * live
    col_acc[b] = col_acc[b] + jnp.sum(both.reshape(16, 8, LANES), axis=0) * other


def first_sweep_kernel(
    row_plan, col_plan, width, place, tiles, ready, row_spot, col_spot, *rest
):
    n_pieces = len(row_plan) + len(col_plan)
    pieces = rest[:n_pieces]
    (kernel_ref, out_ref, held, held_sems, rows_ref, cols_ref, row_sems, col_sems, vec, norms,
     spread_v, spread_n, row_acc, col_acc) = rest[n_pieces:]
    n_col = rows_ref.shape[0]
    n_row = cols_ref.shape[0]
    copies = [[] for _ in range(STAGES)]
    for k, taken in enumerate(row_plan + col_plan):
        target, sems = (rows_ref, row_sems) if k < len(row_plan) else (cols_ref, col_sems)
        for index, part in taken:
            source = pieces[k] if part is None else pieces[k].at[part]
            copy = pltpu.make_async_copy(source, target.at[index], sems.at[index])
            copies[index * STAGES // n_col].append(copy)
    for copy in copies[0] + copies[1]:
        copy.start()
    row_index = place[0]
    col_index = place[1]
    row_acc[...] = jnp.zeros_like(row_acc)
    col_acc[...] = jnp.zeros_like(col_acc)

    lane = lax.broadcasted_iota(jnp.int32, (LANES, LANES), 0)
    take_v = (lane < 3).astype(jnp.float32).astype(jnp.bfloat16)
    take_n = ((lane >= 3) & (lane < 6)).astype(jnp.float32).astype(jnp.bfloat16)
    lane = lax.broadcasted_iota(jnp.int32, (16, LANES), 1)
    line = lax.broadcasted_iota(jnp.int32, (16, LANES), 0)
    take_both = (lane // 3 == line).astype(jnp.float32).astype(jnp.bfloat16)

    def spread(k):
        extra = rows_ref[k, :, width : width + LANES]
        spread_v[k] = jnp.dot(extra, take_v, preferred_element_type=jnp.float32)
        spread_n[k] = jnp.dot(extra, take_n, preferred_element_type=jnp.float32)
        both = lax.dot_general(
            take_both, cols_ref[k, :, width : width + LANES], (((1,), (1,)), ((), ())),
            preferred_element_type=jnp.float32,
        )
        vec[k : k + 1, :] = both[0:1, :]
        norms[k : k + 1, :] = both[1:2, :]

    def save(turn):
        at = pl.ds(turn * GROUP, GROUP)
        return pltpu.make_async_copy(held.at[at], kernel_ref.at[at], held_sems.at[turn])

    def step(turn, carry):
        for g in range(GROUP):
            slot = turn * GROUP + g
            a = row_spot[tiles[slot, 0]]
            b = col_spot[tiles[slot, 1]]
            inner = lax.dot_general(
                rows_ref[a, :, 0:width], cols_ref[b, :, 0:width], (((1,), (1,)), ((), ())),
                preferred_element_type=jnp.float32,
            )
            distance = spread_n[a] + norms[pl.ds(b, 1), :] - 2.0 * inner
            kernel = jnp.exp(jnp.maximum(distance, 0.0) * (-1.0 / width))
            held[slot] = kernel
            add_tile(
                kernel, slot, spread_v[a], vec[pl.ds(b, 1), :], row_acc, col_acc,
                (row_index, col_index), tiles, n_col,
            )
        save(turn).start()
        return carry

    turns = tiles.shape[0] // GROUP
    done = 0
    for stage in range(STAGES):
        for copy in copies[stage]:
            copy.wait()
        if stage + 2 < STAGES:
            for copy in copies[stage + 2]:
                copy.start()
        for k in range(n_col * stage // STAGES, n_col * (stage + 1) // STAGES):
            spread(k)
        upto = ready[stage] if stage + 1 < STAGES else turns
        lax.fori_loop(done, upto, step, 0)
        done = upto
    write_slots(row_acc, col_acc, row_index, col_index, n_row, n_col, out_ref)
    for turn in range(turns):
        save(turn).wait()


def second_sweep_kernel(
    place, tiles, kernel_ref, known_ref, out_ref, own_ref,
    held, held_sems, start_ref, image_ref, next_dir, sums, spread_v, row_acc, col_acc,
    *, n_row, n_col,
):
    fetch = pltpu.make_async_copy(kernel_ref, held, held_sems.at[0])
    fetch.start()
    row_index = place[0]
    col_index = place[1]
    image = known_ref[:, 0:LANES]
    start = known_ref[:, LANES : 2 * LANES]
    image_ref[...] = image
    start_ref[...] = start
    norm_0 = jnp.sum(start * start)
    alpha = norm_0 / jnp.sum(start * image)
    residual = start - alpha * image
    norm_1 = jnp.sum(residual * residual)
    direction = residual + (norm_1 / norm_0) * start
    next_dir[...] = direction
    first = pl.multiple_of(row_index * n_col, n_col)
    spread_columns(next_dir[pl.ds(first, n_col), :], spread_v)
    row_acc[...] = jnp.zeros_like(row_acc)
    col_acc[...] = jnp.zeros_like(col_acc)

    fetch.wait()

    def step(turn, carry):
        for g in range(GROUP):
            slot = turn * GROUP + g
            j = tiles[slot, 1] * n_col + col_index
            add_tile(
                held[slot], slot, spread_v[tiles[slot, 0]], next_dir[pl.ds(j, 1), :],
                row_acc, col_acc,
                (row_index, col_index), tiles, n_col,
            )
        return carry

    lax.fori_loop(0, tiles.shape[0] // GROUP, step, 0)
    write_slots(row_acc, col_acc, row_index, col_index, n_row, n_col, sums)
    partial = jnp.sum(sums[...] * next_dir[...])
    out_ref[:, 0:LANES] = sums[...]
    out_ref[:, LANES : 2 * LANES] = jnp.full((n_row * n_col, LANES), partial, jnp.float32)
    mine = pl.ds(row_index * n_col + col_index, 1)
    own_start = start_ref[mine, :]
    own_dir = next_dir[mine, :]
    own_ref[0:1, :] = alpha * own_start
    own_ref[1:2, :] = own_start - alpha * image_ref[mine, :]
    own_ref[2:3, :] = own_dir
    own_ref[3:4, :] = jnp.full((1, LANES), norm_1, jnp.float32)
    own_ref[4:5, :] = jnp.full((1, LANES), jnp.sum(direction * direction), jnp.float32)
    own_ref[5:8, :] = jnp.zeros((3, LANES), jnp.float32)


def image_kernel(place, partial_ref, own_ref, out_ref, *, block):
    total = jnp.sum(partial_ref[...], axis=0, keepdims=True)
    image = RIDGE * own_ref[...] + total * (1.0 / block)
    both = jnp.concatenate([image, own_ref[...]], axis=1)
    out_ref[...] = jnp.broadcast_to(both, out_ref.shape)


def finish_kernel(partial_ref, own_ref, solution_ref, residual_ref, *, block):
    total = jnp.sum(partial_ref[...], axis=0, keepdims=True)
    direction = own_ref[2:3, :]
    image = RIDGE * direction + total[:, 0:LANES] * (1.0 / block)
    against = RIDGE * own_ref[4:5, :] + total[:, LANES : 2 * LANES] * (1.0 / block)
    alpha = own_ref[3:4, :] / against
    solution_ref[...] = own_ref[0:1, :] + alpha * direction
    residual_ref[...] = own_ref[1:2, :] - alpha * image


def in_order(pairs, count, row_spot, col_spot):
    slots = pairs.shape[0]
    spots_of = jnp.arange(row_spot.shape[0], dtype=jnp.int32)[None, :]
    row_at = jnp.sum(jnp.where(pairs[:, 0:1] == spots_of, row_spot[None, :], 0), axis=1)
    col_at = jnp.sum(jnp.where(pairs[:, 1:2] == spots_of, col_spot[None, :], 0), axis=1)
    slot = jnp.arange(slots, dtype=jnp.int32)
    arrival = jnp.maximum(row_at, col_at)
    key = arrival * slots + slot
    rank = jnp.sum((key[None, :] < key[:, None]).astype(jnp.int32), axis=1)
    known = jnp.stack([pairs[:, 0], pairs[:, 1], (slot < count).astype(jnp.int32)], axis=1)
    chosen = rank[None, :] == slot[:, None]
    tiles = jnp.sum(jnp.where(chosen[:, :, None], known[None, :, :], 0), axis=1)
    fetched = (jnp.arange(STAGES, dtype=jnp.int32) + 1) * (row_spot.shape[0] // STAGES)
    ready = jnp.sum((arrival[None, :] < fetched[:, None]).astype(jnp.int32), axis=1) // GROUP
    return tiles, ready


def swap(slots):
    return lax.all_to_all(slots, AXES, 0, 0, tiled=True)


VM = pl.BlockSpec(memory_space=pltpu.VMEM)
SM = pl.BlockSpec(memory_space=pltpu.SMEM)
HB = pl.BlockSpec(memory_space=pltpu.HBM)
NX, NZ = 4, 4
NY, NH, NK = 4, 2, 2


def coords(device):
    row, col = divmod(device, NX * NZ)
    return row // 4, row // 2 % 2, row % 2, col // NZ, col % NZ


def device_at(y, half, core, x, z):
    return ((y % NY * NH + half) * NK + core) * NX * NZ + x % NX * NZ + z


def send(array, move):
    pairs = [(d, device_at(*move(*coords(d)))) for d in range(NY * NH * NK * NX * NZ)]
    return lax.ppermute(array, AXES, pairs)


def along_z(array, bit, only=range(NZ)):
    pairs = []
    for d in range(NY * NH * NK * NX * NZ):
        y, h, k, x, z = coords(d)
        if z in only:
            pairs.append((d, device_at(y, h, k, x, z ^ bit)))
    return lax.ppermute(array, AXES, pairs)


def along_x(array, step):
    return send(array, lambda y, h, k, x, z: (y, h, k, x + (step if k == 0 else -step), z))


def along_y(array, step):
    return send(array, lambda y, h, k, x, z: (y + (step if k == 0 else -step), h, k, x, z))


def across(array):
    return send(array, lambda y, h, k, x, z: (y, 1 - h, k, x, z))


def sibling(array):
    return send(array, lambda y, h, k, x, z: (y, h, 1 - k, x, z))


def together(*arrays):
    return lax.optimization_barrier(arrays[::-1])[::-1]


def gather(mine, small):
    z = lax.axis_index("col") % NZ
    middle = (z == 1) | (z == 2)
    inside = (1, 2)

    z3, z1 = along_z(mine, 3), along_z(mine, 1)
    one, two = along_x(mine, 1), along_x(mine, -1)
    near, back = along_y(mine, 1), along_y(mine, -1)
    z3, z1, one, two, near, back = together(z3, z1, one, two, near, back)

    over = across(mine)
    z13 = jnp.stack([z1, z3])
    one13, two13 = along_x(z13, 1), along_x(z13, -1)
    inner, outer = along_z(z1, 3, inside), along_z(z3, 1, inside)
    far, rim = along_x(one, 1), along_y(near, 1)
    over, one13, two13, inner, outer, far, rim = together(
        over, one13, two13, inner, outer, far, rim
    )

    z2 = jnp.where(middle, inner, outer)
    far13, one2, two2 = along_x(one13, 1), along_x(z2, 1), along_x(z2, -1)
    near_c, back_c = along_y(over, 1), along_y(over, -1)
    line = jnp.stack([mine, near, rim, back])
    far13, one2, two2, near_c, back_c, line, *small = together(
        far13, one2, two2, near_c, back_c, line, *small
    )

    far2, rim_c = along_x(one2, 1), along_y(near_c, 1)
    twin, twin_c = sibling(line), sibling(jnp.stack([over, near_c, back_c]))
    rim_c, far2, twin, twin_c = together(rim_c, far2, twin, twin_c)

    rim_twin = sibling(rim_c)

    rows = [mine, one, far, two, z13, one13, far13, two13, z2, one2, far2, two2]
    row_plan = [((NZ * turn, None),) for turn in range(NX)]
    row_plan += [((NZ * turn + 1, 0), (NZ * turn + 2, 1)) for turn in range(NX)]
    row_plan += [((NZ * turn + 3, None),) for turn in range(NX)]
    cols = [line, over, near_c, rim_c, back_c, twin, twin_c, rim_twin]
    col_plan = [tuple((k, k) for k in range(NY))] + [((k, None),) for k in range(NY, 2 * NY)]
    col_plan += [tuple((8 + k, k) for k in range(NY)), ((12, 0), (13, 1), (15, 2)), ((14, None),)]
    return rows, row_plan, cols, col_plan, small


def spots():
    total = NY * NH * NK * NX * NZ
    row_spot = np.zeros((total, NX * NZ), np.int32)
    col_spot = np.zeros((total, NY * NH * NK), np.int32)
    for d in range(total):
        y, h, k, x, z = coords(d)
        sign = 1 if k == 0 else -1
        order = [z, z ^ 1, z ^ 3, z ^ 2]
        for a in range(NX * NZ):
            turn = sign * (x - a // NZ) % NX
            row_spot[d, a] = NZ * turn + order.index(a % NZ)
        for b in range(NY * NH * NK):
            swap_k = (b ^ k) & 1
            turn = (-sign if swap_k else sign) * (y - b // 4) % NY
            col_spot[d, b] = 8 * swap_k + 4 * ((b // 2 ^ h) & 1) + turn
    here = lax.axis_index("row") * NX * NZ + lax.axis_index("col")
    return jnp.asarray(row_spot)[here], jnp.asarray(col_spot)[here]


def body(features, targets, tile_pairs, tile_count):
    n_row = lax.axis_size("row")
    n_col = lax.axis_size("col")
    total = n_row * n_col
    place = jnp.stack([lax.axis_index("row"), lax.axis_index("col")]).astype(jnp.int32)
    pairs = tile_pairs[0, 0]
    count = tile_count[0, 0]
    slots = pairs.shape[0]
    block, width = features.shape
    params = pltpu.CompilerParams(vmem_limit_bytes=SMALL)
    f32 = jnp.float32

    packed = pl.pallas_call(
        pack_kernel,
        out_shape=jax.ShapeDtypeStruct((block, width + LANES), jnp.bfloat16),
        in_specs=[VM, VM],
        out_specs=VM,
        compiler_params=params,
    )(features, targets[None, :])
    row_spot, col_spot = spots()
    tiles, ready = in_order(pairs, count, row_spot, col_spot)
    small = (place, tiles, ready, row_spot, col_spot)
    row_pieces, row_plan, col_pieces, col_plan, small = gather(packed, small)
    place, tiles, ready, row_spot, col_spot = small

    accumulators = [
        pltpu.VMEM((n_col, block, block), f32),
        pltpu.VMEM((n_row, 8, block), f32),
    ]
    kernel, partial = pl.pallas_call(
        lambda *refs: first_sweep_kernel(row_plan, col_plan, width, *refs),
        out_shape=(
            jax.ShapeDtypeStruct((slots, block, block), f32),
            jax.ShapeDtypeStruct((total, block), f32),
        ),
        in_specs=[SM, SM, SM, SM, SM] + [HB] * (len(row_plan) + len(col_plan)),
        out_specs=(HB, VM),
        scratch_shapes=[
            pltpu.VMEM((slots, block, block), f32),
            pltpu.SemaphoreType.DMA((slots // GROUP,)),
            pltpu.VMEM((n_col, block, width + LANES), jnp.bfloat16),
            pltpu.VMEM((n_row, block, width + LANES), jnp.bfloat16),
        ]
        + [pltpu.SemaphoreType.DMA((n_col,)), pltpu.SemaphoreType.DMA((n_row,))]
        + [pltpu.VMEM((n_row, block), f32)] * 2
        + [pltpu.VMEM((n_col, block, block), f32)] * 2 + accumulators,
        compiler_params=pltpu.CompilerParams(vmem_limit_bytes=LARGE),
    )(place, tiles, ready, row_spot, col_spot, *row_pieces, *col_pieces)

    image = pl.pallas_call(
        lambda *refs: image_kernel(None, *refs, block=block),
        out_shape=jax.ShapeDtypeStruct((total, 2 * block), f32),
        in_specs=[VM, VM],
        out_specs=VM,
        compiler_params=params,
    )(swap(partial), targets[None, :])
    images = swap(image)

    partial_2, own = pl.pallas_call(
        lambda *refs: second_sweep_kernel(*refs, n_row=n_row, n_col=n_col),
        out_shape=(
            jax.ShapeDtypeStruct((total, 2 * block), f32),
            jax.ShapeDtypeStruct((8, block), f32),
        ),
        in_specs=[SM, SM, HB, VM],
        out_specs=(VM, VM),
        scratch_shapes=[
            pltpu.VMEM((slots, block, block), f32),
            pltpu.SemaphoreType.DMA((1,)),
            pltpu.VMEM((total, block), f32),
            pltpu.VMEM((total, block), f32),
            pltpu.VMEM((total, block), f32),
            pltpu.VMEM((total, block), f32),
            pltpu.VMEM((n_col, block, block), f32),
        ] + accumulators,
        compiler_params=params,
    )(place, tiles, kernel, images)

    result, residual = pl.pallas_call(
        lambda *refs: finish_kernel(*refs, block=block),
        out_shape=(jax.ShapeDtypeStruct((1, block), f32),) * 2,
        in_specs=[VM, VM],
        out_specs=(VM, VM),
        compiler_params=params,
    )(swap(partial_2), own)
    return (result[0], residual[0])


def solution(mesh):
    return jax.shard_map(
        body,
        mesh=mesh,
        in_specs=(
            P(("row", "col"), None),
            P(("row", "col")),
            P("row", "col", None, None),
            P("row", "col"),
        ),
        out_specs=(P(("row", "col")), P(("row", "col"))),
        check_vma=False,
    )
```
